128 devices in a mesh: expert: 16 (over x, y_lo, core), dp: 8 (over y_hi, z).
Axes of the slice: x: 4, y: 4 (y_hi: 2, y_lo: 2; y = y_hi * 2 + y_lo), z: 4, core: 2. Of those that a mesh axis runs over, the one named last changes fastest.
Arguments:
- tokens: bfloat16 [8, 8192, 2048], P('dp', 'expert'), may hold values from -6 to 6
- cotangent: bfloat16 [8, 8192, 2048], P('dp', 'expert'), may hold values from -0.09375 to 0.09375
- routes: int32 [8, 8192, 1], P('dp', 'expert'), may hold values from 0 to 15; in each aligned block of 512 rows (0 to 511, 512 to 1023, ..., all dimensions but the last counted through in order) at most 64 rows name the same one
- owner: int32 [16], replicated, may hold values from 0 to 15, as said below
- master: float32 [16, 2048, 2304], P('expert', 'dp'), may hold values from -0.125 to 0.125
- moment1: float32 [16, 2048, 2304], P('expert', 'dp'), may hold values from -1.8 to 1.8
- moment2: float32 [16, 2048, 2304], P('expert', 'dp'), may hold values from 0.01 to 1
Outputs:
- token_grad: bfloat16 [8, 8192, 2048], P('dp', 'expert')
- new_master: float32 [16, 2048, 2304], P('expert', 'dp')
- new_moment1: float32 [16, 2048, 2304], P('expert', 'dp')
- new_moment2: float32 [16, 2048, 2304], P('expert', 'dp')
The draws below stay inside these ranges and needn't reach their ends.
Inputs may be any that keep to these rules, and one draw needn't show every extreme that they name: owner[j] is j or j xor (8), and owner[j] == j exactly when the same holds for j xor (8); at least one pair moves. `routes`: among the 512 tokens of one device at most 64 choose one expert, and some expert is chosen by exactly 64.
All inputs are finite; a program needn't handle non-finite values.
Results may differ from the reference program's by a relative error of at most 0.012.
Values may be sent and summed in bfloat16 or wider, within the bound.
No kernel may reach another device: no remote copies, remote signals or barrier semaphores. Data moves between devices by JAX's collectives and lax.ppermute only.
A program may use at most 128 MiB of HBM per device.

```python
import math
import jax
import jax.numpy as jnp
import numpy as np
from jax import lax

D = 2048
HID = 768
TOK_DEV = 512
EXPERTS = 16
CAP = 64
N_EXPERT = 16
N_DP = 8


def draw_owner(key, part):
    key = jax.random.fold_in(key, 7)
    half = EXPERTS // 2
    flips = jax.random.randint(key, (half,), 0, 2)
    forced = jax.random.randint(jax.random.fold_in(key, 1), (), 0, half)
    flips = jnp.where(jnp.arange(half) == forced, 1, flips)
    index = jnp.arange(EXPERTS, dtype=jnp.int32)
    moved = flips[index % half]
    return jnp.where(moved == 1, jnp.bitwise_xor(index, half), index).astype(jnp.int32)


def level_of(key, extent, split, smallest, largest):
    def one(position, parts):
        heights = jax.random.uniform(jax.random.fold_in(jax.random.fold_in(key, 6), position), (parts,), jnp.float32, smallest / len(split), largest / len(split))
        return jnp.repeat(jnp.exp(heights), extent[position] // parts).reshape((-1,) + (1,) * (len(extent) - position - 1))

    loudness = one(*split[0])
    for cut in split[1:]:
        loudness = loudness * one(*cut)
    return loudness


def assign_block(stream_key, own, number, rows, amount, top, limit, skew):
    sequence = jax.random.permutation(stream_key, amount)
    heavy_load, usual = shares(amount, rows * top, limit, skew, True), shares(amount, rows * top, limit, skew, False)
    places = jnp.arange(amount)

    def named(tallies, offset_by):
        used = int((tallies > 0).sum())
        fixed = max(1, used // 4)
        moved = fixed + (places - fixed + offset_by * (used - fixed)) % max(1, amount - fixed)
        return jnp.zeros((amount,), jnp.int32).at[sequence[jnp.where(places < fixed, places, moved)]].set(jnp.asarray(tallies, jnp.int32))

    tallies = jnp.where(number % 4 == 0, named(heavy_load, number // 4), named(usual, number - number // 4 - 1))
    mixed = jax.random.permutation(jax.random.fold_in(own, 3), amount)
    donor, receiver = mixed[0:amount // 2 * 2:2], mixed[1:amount // 2 * 2:2]
    margin = jnp.minimum(tallies[donor] - 1, limit - tallies[receiver]) // 2
    margin = jnp.where((donor == sequence[0]) | (receiver == sequence[0]) | (tallies[receiver] == 0), 0, jnp.maximum(margin, 0))
    moved = jax.random.randint(jax.random.fold_in(own, 4), (amount // 2,), 0, 1 << 20) % (margin + 1)
    tallies = tallies.at[donor].add(-moved).at[receiver].add(moved)
    members = jnp.searchsorted(jnp.cumsum(tallies), jnp.arange(rows * top), side="right").astype(jnp.int32)
    grid = members.reshape(top, rows).T
    grid = grid[jax.random.permutation(jax.random.fold_in(own, 1), rows)]
    offset_by = jax.random.randint(jax.random.fold_in(own, 2), (rows, 1), 0, top)
    return jnp.take_along_axis(grid, (jnp.arange(top)[None, :] + offset_by) % top, axis=1)


def shares(number_of, total, limit, lean, full):
    loads = [(1 << 20) // math.isqrt(rank ** lean) + 1 for rank in range(1, number_of + 1)]
    largest = limit if full else min(limit, max(-(-total // number_of), total * loads[0] // sum(loads)))
    least = 1 if total - largest >= number_of - 1 else 0
    holding, surplus = [largest] + [least] * (number_of - 1), total - largest - least * (number_of - 1)
    while surplus > 0:
        free = [i for i in range(1, number_of) if holding[i] < largest] or [i for i in range(1, number_of) if holding[i] < limit]
        mass, left = sum([loads[i] for i in free]), surplus
        for i in free:
            extra = min(limit - holding[i], max(1, left * loads[i] // mass), surplus)
            holding[i] = holding[i] + extra
            surplus = surplus - extra
    return np.array(holding)


def noise(stream_key, extent, spread, limit, pieces=(), kind=jnp.bfloat16):
    drawn = spread * jax.random.normal(stream_key, extent, jnp.float32)
    if pieces:
        drawn = drawn * level_of(stream_key, extent, pieces, -0.22, 0.18)
    return jnp.clip(drawn, -limit, limit).astype(kind)


def setup_inputs(seed: int = 0) -> dict:
    seeds = jax.random.split(jax.random.key(seed), 8)
    tokens = noise(seeds[0], (N_DP, N_EXPERT * TOK_DEV, D), 1.0, 6.0, ((0, 8), (1, 16)))
    cotangent = noise(seeds[1], (N_DP, N_EXPERT * TOK_DEV, D), (1.0 / (TOK_DEV * N_DP) ** 0.5), 0.09375, ((0, 8), (1, 16)))
    routes_keys = jax.random.split(jax.random.fold_in(seeds[2], 1), N_DP * (N_EXPERT * TOK_DEV) // TOK_DEV)
    routes_turns = jax.random.permutation(jax.random.fold_in(seeds[2], 3), N_DP * (N_EXPERT * TOK_DEV) // TOK_DEV)
    routes = jax.vmap(lambda own, number: assign_block(jax.random.fold_in(seeds[2], 2), own, number, TOK_DEV, N_EXPERT, 1, CAP, 2))(routes_keys, routes_turns).reshape((N_DP, N_EXPERT * TOK_DEV, 1))
    owner = draw_owner(jax.random.fold_in(seeds[7], 71), 0)
    master = noise(seeds[4], (EXPERTS, D, 3 * HID), D ** -0.5, 0.125, ((0, 16), (1, 8)), jnp.float32)
    moment1 = noise(seeds[5], (EXPERTS, D, 3 * HID), 0.3, 1.8, ((0, 16), (1, 8)), jnp.float32)
    moment2 = jnp.clip(jnp.exp(math.log(1.0) - 4.6051702 * jax.random.uniform(seeds[6], (EXPERTS, D, 3 * HID), jnp.float32) ** level_of(seeds[6], (EXPERTS, D, 3 * HID), ((0, 16), (1, 8)), -0.2, 0.2)), 0.01, 1.0)
    return {"tokens": tokens, "cotangent": cotangent, "routes": routes, "owner": owner, "master": master, "moment1": moment1, "moment2": moment2}


def reference(tokens, cotangent, routes, owner, master, moment1, moment2):
    half = EXPERTS // 2
    ids = jnp.arange(EXPERTS, dtype=jnp.int32)
    source = jnp.where(owner == ids, ids, jnp.bitwise_xor(ids, half)).astype(jnp.int32)
    placed_master = master[source]
    placed_first = moment1[source]
    placed_second = moment2[source]
    weights = placed_master.astype(jnp.bfloat16).astype(jnp.float32)
    gate_up = weights[:, :, :2 * HID]
    down = weights[:, :, 2 * HID:]

    def group(total, inputs):
        x_group, dy_group, route_group = inputs
        route_pos = route_group.reshape(EXPERTS, TOK_DEV)
        onehot = (route_pos[:, :, None] == ids[None, None, :]).astype(jnp.int32)
        slot = lax.optimization_barrier(jnp.sum((jnp.cumsum(onehot, axis=1) - 1) * onehot, axis=2))
        anchor = jnp.arange(EXPERTS, dtype=jnp.int32)[:, None]
        flat = (route_pos * (EXPERTS * CAP) + anchor * CAP + slot).reshape(-1).astype(jnp.int32)
        box_x = jnp.zeros((EXPERTS * EXPERTS * CAP, D), jnp.bfloat16).at[flat].set(x_group)
        box_dy = jnp.zeros((EXPERTS * EXPERTS * CAP, D), jnp.bfloat16).at[flat].set(dy_group)
        rows_x = box_x.reshape(EXPERTS, EXPERTS * CAP, D).astype(jnp.float32)
        rows_dy = box_dy.reshape(EXPERTS, EXPERTS * CAP, D).astype(jnp.float32)
        pre = jnp.einsum('erd,edk->erk', rows_x, gate_up)
        gate_pre = pre[:, :, :HID]
        up_pre = pre[:, :, HID:]
        sig = jax.nn.sigmoid(gate_pre)
        act = gate_pre * sig
        hidden = (act * up_pre).astype(jnp.bfloat16).astype(jnp.float32)
        d_hidden = jnp.einsum('erd,edk->erk', rows_dy, down)
        d_gate = (d_hidden * up_pre * sig * (1.0 + gate_pre * (1.0 - sig))).astype(jnp.bfloat16)
        d_up = (d_hidden * act).astype(jnp.bfloat16)
        d_both = jnp.concatenate([d_gate, d_up], axis=2).astype(jnp.float32)
        part_gu = jnp.einsum('erd,erk->edk', rows_x, d_both)
        part_down = jnp.einsum('erd,erk->edk', rows_dy, hidden)
        partial_value = jnp.concatenate([part_gu, part_down], axis=2).astype(jnp.bfloat16)
        in_grad = jnp.einsum('erk,edk->erd', d_both, gate_up).astype(jnp.bfloat16)
        token_rows = in_grad.reshape(EXPERTS * EXPERTS * CAP, D)[flat]
        return (total + partial_value.astype(jnp.float32), token_rows)
    start = jnp.zeros((EXPERTS, D, 3 * HID), jnp.float32)
    grad, token_grad = lax.scan(group, start, (tokens, cotangent, routes[:, :, 0]))
    new_first = 0.9 * placed_first + 0.1 * grad
    new_second = 0.95 * placed_second + 0.05 * grad * grad
    step = new_first / (1.0 - 0.9 ** 10) / (jnp.sqrt(new_second / (1.0 - 0.95 ** 10)) + 1e-08)
    new_master = placed_master - 0.003 * (step + 0.1 * placed_master)
    return (token_grad, new_master, new_first, new_second)
```

```python
import functools
import jax
import jax.numpy as jnp
from jax import lax
from jax.experimental import pallas as pl
from jax.experimental.pallas import tpu as pltpu
from jax.sharding import PartitionSpec as P

BF = jnp.bfloat16
F32 = jnp.float32
VMEM_LIMIT = 56 * 1024 * 1024
ZN = 4


def params():
    return pltpu.CompilerParams(vmem_limit_bytes=VMEM_LIMIT)


def cost(flops, nbytes):
    return pl.CostEstimate(flops=int(flops), bytes_accessed=int(nbytes), transcendentals=0)


def permuted(value, axis, target):
    return lax.ppermute(value, axis, [(i, target(i)) for i in range(lax.axis_size(axis))])


def mm(a, b, dims):
    return lax.dot_general(a, b, (dims, ((), ())), preferred_element_type=F32)


def dispatch_kernel(flat_ref, tok_ref, out_ref, onehot_ref):
    @pl.when(pl.program_id(0) == 0)
    def _():
        rows, count = onehot_ref.shape
        ids = lax.broadcasted_iota(jnp.int32, (rows, count), 0)
        onehot_ref[...] = (ids == flat_ref[...]).astype(F32).astype(BF)

    out_ref[...] = mm(onehot_ref[...], tok_ref[...], ((1,), (0,))).astype(BF)


def dispatch(flat, tok, rows, first, blocks, place):
    count, features = tok.shape
    width = features // (2 * ZN)
    return pl.pallas_call(
        dispatch_kernel,
        grid=(blocks,),
        in_specs=[
            pl.BlockSpec((1, count), lambda i: (0, 0)),
            pl.BlockSpec((count, width), lambda i: (0, first + i)),
        ],
        out_specs=pl.BlockSpec((rows, width), lambda i: (0, place(i))),
        out_shape=jax.ShapeDtypeStruct((rows, blocks * width), BF),
        scratch_shapes=[pltpu.VMEM((rows, count), BF)],
        compiler_params=params(),
        cost_estimate=cost(2 * rows * count * blocks * width, 2 * blocks * width * (rows + count)),
        name="dispatch",
    )(flat.reshape(1, count), tok)


def combine_kernel(flat_ref, back_ref, out_ref, onehot_ref):
    @pl.when(pl.program_id(0) == 0)
    def _():
        count, rows = onehot_ref.shape
        ids = lax.broadcasted_iota(jnp.int32, (count, rows), 1)
        onehot_ref[...] = (ids == flat_ref[...]).astype(F32).astype(BF)

    out_ref[...] = mm(onehot_ref[...], back_ref[...], ((1,), (0,))).astype(BF)


def combine(flat, back, count):
    rows, features = back.shape
    groups = 2 * ZN
    width = features // groups
    return pl.pallas_call(
        combine_kernel,
        grid=(groups,),
        in_specs=[
            pl.BlockSpec((count, 1), lambda i: (0, 0)),
            pl.BlockSpec((rows, width), lambda i: (0, (i % ZN) * 2 + i // ZN)),
        ],
        out_specs=pl.BlockSpec((count, width), lambda i: (0, i)),
        out_shape=jax.ShapeDtypeStruct((count, features), BF),
        scratch_shapes=[pltpu.VMEM((count, rows), BF)],
        compiler_params=params(),
        cost_estimate=cost(2 * rows * count * features, 2 * features * (rows + count)),
        name="combine",
    )(flat.reshape(count, 1), back)


def forward_kernel(x_ref, gate_ref, up_ref, h_ref, p_ref, s_ref):
    x = x_ref[...]
    g = mm(x, gate_ref[...], ((1,), (0,)))
    u = mm(x, up_ref[...], ((1,), (0,)))
    sig = jax.nn.sigmoid(g)
    s = g * sig
    h_ref[...] = (s * u).astype(BF)
    p_ref[...] = u * sig * (1.0 + g * (1.0 - sig))
    s_ref[...] = s


def forward(x, gate_up):
    rows, features = x.shape
    hidden = gate_up.shape[1] // 2
    tile = min(256, hidden)
    tiles = hidden // tile
    out = pl.BlockSpec((rows, tile), lambda j: (0, j))
    return pl.pallas_call(
        forward_kernel,
        grid=(hidden // tile,),
        in_specs=[
            pl.BlockSpec((rows, features), lambda j: (0, 0)),
            pl.BlockSpec((features, tile), lambda j: (0, j)),
            pl.BlockSpec((features, tile), lambda j: (0, j + tiles)),
        ],
        out_specs=[out, out, out],
        out_shape=[
            jax.ShapeDtypeStruct((rows, hidden), BF),
            jax.ShapeDtypeStruct((rows, hidden), F32),
            jax.ShapeDtypeStruct((rows, hidden), F32),
        ],
        compiler_params=params(),
        cost_estimate=cost(4 * rows * features * hidden, 20e6),
        name="forward",
    )(x, gate_up, gate_up)


def hidden_first_kernel(dy_ref, down_ref, dh_ref):
    dh_ref[...] = mm(dy_ref[...], down_ref[...], ((1,), (0,)))


def hidden_kernel(dy_ref, down_ref, dh_ref, p_ref, s_ref, dg_ref, du_ref):
    dh = dh_ref[...] + mm(dy_ref[...], down_ref[...], ((1,), (0,)))
    dg_ref[...] = (dh * p_ref[...]).astype(BF)
    du_ref[...] = (dh * s_ref[...]).astype(BF)


def hidden_call(kernel, dy, down, more, outs, name):
    rows, features = dy.shape
    hidden = down.shape[1]
    tile = min(256, hidden)
    out = pl.BlockSpec((rows, tile), lambda j: (0, j))
    return pl.pallas_call(
        kernel,
        grid=(hidden // tile,),
        in_specs=[
            pl.BlockSpec((rows, features), lambda j: (0, 0)),
            pl.BlockSpec((features, tile), lambda j: (0, j)),
        ]
        + [out] * len(more),
        out_specs=[out] * len(outs),
        out_shape=[jax.ShapeDtypeStruct((rows, hidden), t) for t in outs],
        compiler_params=params(),
        cost_estimate=cost(2 * rows * features * hidden, 17e6),
        name=name,
    )(dy, down, *more)


def weight_kernel(a_ref, b_ref, out_ref):
    out_ref[...] = mm(a_ref[...], b_ref[...], ((0,), (0,))).astype(BF)


def weight_grad(a, b, name):
    rows, features = a.shape
    hidden = b.shape[1]
    tile = 512
    return pl.pallas_call(
        weight_kernel,
        grid=(features // tile,),
        in_specs=[
            pl.BlockSpec((rows, tile), lambda i: (0, i)),
            pl.BlockSpec((rows, hidden), lambda i: (0, 0)),
        ],
        out_specs=pl.BlockSpec((tile, hidden), lambda i: (i, 0)),
        out_shape=jax.ShapeDtypeStruct((features, hidden), BF),
        compiler_params=params(),
        cost_estimate=cost(2 * rows * features * hidden, 9e6),
        name=name,
    )(a, b)


def input_kernel(dg_ref, du_ref, gate_ref, up_ref, out_ref):
    acc = mm(dg_ref[...], gate_ref[...], ((1,), (1,)))
    acc = acc + mm(du_ref[...], up_ref[...], ((1,), (1,)))
    out_ref[...] = acc.astype(BF)


def input_grad(dg, du, gate_up):
    rows, hidden = dg.shape
    features = gate_up.shape[0]
    tile = 512
    left = pl.BlockSpec((rows, hidden), lambda i: (0, 0))
    gate = pl.BlockSpec((tile, hidden), lambda i: (i, 0))
    up = pl.BlockSpec((tile, hidden), lambda i: (i, 1))
    return pl.pallas_call(
        input_kernel,
        grid=(features // tile,),
        in_specs=[left, left, gate, up],
        out_specs=pl.BlockSpec((rows, tile), lambda i: (0, i)),
        out_shape=jax.ShapeDtypeStruct((rows, features), BF),
        compiler_params=params(),
        cost_estimate=cost(4 * rows * features * hidden, 14e6),
        name="input_grad",
    )(dg, du, gate_up, gate_up)


def adam_kernel(info_ref, own_ref, far_ref, w_ref, m_ref, v_ref, wb_ref, mb_ref, vb_ref, *rest):
    nw_ref, nm_ref, nv_ref = rest[-3:]
    keep = info_ref[0] != 0
    grad = own_ref[...].astype(F32) + far_ref[...].astype(F32)
    w = jnp.where(keep, w_ref[...], wb_ref[...].astype(F32))
    m = jnp.where(keep, m_ref[...], mb_ref[...].astype(F32))
    v = jnp.where(keep, v_ref[...], vb_ref[...].astype(F32))
    m = 0.9 * m + 0.1 * grad
    v = 0.95 * v + 0.05 * grad * grad
    update = m / (1.0 - 0.9**10) / (jnp.sqrt(v / (1.0 - 0.95**10)) + 1e-08)
    nw_ref[...] = w - 0.003 * (update + 0.1 * w)
    nm_ref[...] = m
    nv_ref[...] = v


def adam(info, near, far, state, moved, k, before):
    rows, hidden = far.shape
    tile = min(64, rows)
    chunk = pl.BlockSpec((tile, hidden), lambda i, info: (i, 0))
    column = pl.BlockSpec((tile, hidden), lambda i, info: (i, k))
    shape = jax.ShapeDtypeStruct(state[0].shape, F32)
    return pl.pallas_call(
        adam_kernel,
        grid_spec=pltpu.PrefetchScalarGridSpec(
            num_scalar_prefetch=1,
            grid=(rows // tile,),
            in_specs=[chunk, chunk]
            + [column] * 3
            + [chunk] * 3
            + [pl.BlockSpec(memory_space=pl.ANY)] * len(before),
            out_specs=[column] * 3,
        ),
        out_shape=[shape] * 3,
        input_output_aliases={9 + i: i for i in range(len(before))},
        compiler_params=params(),
        cost_estimate=cost(20 * rows * hidden, 34 * rows * hidden),
        name="adam",
    )(info, near, far, *state, *moved, *before)


def per_device(tokens, cotangent, routes, owner, master, moment1, moment2):
    experts = lax.axis_size("expert")
    half = experts // 2
    position = lax.axis_index("expert")
    high = lax.axis_index("dp") // ZN
    keep = owner[position] == position
    info = keep.astype(jnp.int32).reshape(1)
    hidden = master.shape[2] // 3
    features = tokens.shape[2]
    count = tokens.shape[1]
    capacity = 2 * count // experts
    rows = experts * capacity
    replicas = lax.axis_size("dp")
    z_groups = [[h * ZN + z for z in range(ZN)] for h in range(replicas // ZN)]

    route_ids = routes[0, :, 0]
    columns = jnp.arange(experts, dtype=jnp.int32)
    onehot = (route_ids[:, None] == columns[None, :]).astype(jnp.int32)
    slot = jnp.sum((jnp.cumsum(onehot, axis=0) - 1) * onehot, axis=1)
    flat = route_ids * capacity + slot
    groups = 2 * ZN
    send_x = dispatch(flat, tokens[0], rows, 0, groups, lambda i: (i % ZN) * 2 + i // ZN)
    send_dy = [dispatch(flat, cotangent[0], rows, n * ZN, ZN, lambda i: i) for n in range(2)]

    def over_owners(value):
        return permuted(value, "expert", lambda i: i ^ half)

    def over_high(value):
        return permuted(value, "dp", lambda i: i ^ ZN)

    def over_experts(value):
        boxes = value.reshape(experts, capacity, value.shape[1])
        out = lax.all_to_all(boxes, "expert", split_axis=0, concat_axis=0, tiled=True)
        return out.reshape(value.shape)

    def gathered(value):
        return lax.all_gather(value, "dp", axis=0, tiled=True, axis_index_groups=z_groups)

    def scattered(grad):
        return lax.psum_scatter(
            grad, "dp", scatter_dimension=0, tiled=True, axis_index_groups=z_groups
        )

    def both(near, far):
        return jnp.where(high == 0, near, far), jnp.where(high == 0, far, near)

    split = 2 * hidden
    own_a, own_b = master[0, :, :split].astype(BF), master[0, :, split:].astype(BF)
    other_a = over_owners(own_a)
    own_b, other_a = lax.optimization_barrier((own_b, other_a))
    other_b = over_owners(own_b)
    placed_a = jnp.where(keep, own_a, other_a)
    far_a = over_high(placed_a)
    placed_a, far_a, other_b, send_x = lax.optimization_barrier((placed_a, far_a, other_b, send_x))
    gate_up = gathered(jnp.concatenate(both(placed_a, far_a), axis=0))
    x = over_experts(send_x)
    placed_b = jnp.where(keep, own_b, other_b)
    far_b = over_high(placed_b)
    down = [gathered(v) for v in both(placed_b, far_b)]

    send_first, x = lax.optimization_barrier((send_dy[0], x))
    dy_first = over_experts(send_first)
    h, p, s = forward(x, gate_up)
    send_second, h = lax.optimization_barrier((send_dy[1], h))
    dy_second = over_experts(send_second)
    part_first = scattered(weight_grad(dy_first, h, "grad_down"))
    (dh,) = hidden_call(hidden_first_kernel, dy_first, down[0], [], [F32], "hidden_first")

    m_own, v_own = moment1[0].astype(BF), moment2[0].astype(BF)
    m_own = [m_own[:, :hidden], m_own[:, hidden:]]
    dy_second, *m_own, v_own = lax.optimization_barrier((dy_second, *m_own, v_own))
    m_other = [over_owners(v) for v in m_own]
    v_other = over_owners(v_own)
    part_second = scattered(weight_grad(dy_second, h, "grad_down"))
    dg, du = hidden_call(
        hidden_kernel, dy_second, down[1], [dh, p, s], [BF, BF], "hidden_grads"
    )
    grad, m_other[0] = lax.optimization_barrier((weight_grad(x, dg, "grad_gate"), m_other[0]))
    part_gate = scattered(grad).reshape(2, -1, hidden)
    grad, m_other[1] = lax.optimization_barrier((weight_grad(x, du, "grad_up"), m_other[1]))
    part_up = scattered(grad).reshape(2, -1, hidden)
    near, away = both(part_first, part_second)
    sums = {2: (near, over_high(away))}
    for k, part in ((0, part_gate), (1, part_up)):
        near, away = both(part[0], part[1])
        sums[k] = (near, over_high(away))
    send_back = input_grad(dg, du, gate_up)
    send_back, v_other = lax.optimization_barrier((send_back, v_other))
    token_grad = combine(flat, over_experts(send_back), count)

    m_other = (m_other[0], m_other[1][:, :hidden], m_other[1][:, hidden:])
    other = (other_a[:, :hidden], other_a[:, hidden:], other_b)
    state = (master[0], moment1[0], moment2[0])
    new = ()
    for k in (2, 0, 1):
        near, far = sums[k]
        shifted = (other[k], m_other[k], v_other[:, k * hidden : (k + 1) * hidden])
        new = adam(info, near, far, state, shifted, k, new)
    return (token_grad[None], new[0][None], new[1][None], new[2][None])


def solution(mesh):
    placed = (
        P("dp", "expert", None),
        P("dp", "expert", None),
        P("dp", "expert", None),
        P(),
        P("expert", "dp", None),
        P("expert", "dp", None),
        P("expert", "dp", None),
    )
    return jax.shard_map(
        per_device,
        mesh=mesh,
        in_specs=placed,
        out_specs=(
            P("dp", "expert", None),
            P("expert", "dp", None),
            P("expert", "dp", None),
            P("expert", "dp", None),
        ),
        check_vma=False,
    )
```

```python
import functools
import jax
import jax.numpy as jnp
from jax import lax
from jax.experimental import pallas as pl
from jax.experimental.pallas import tpu as pltpu
from jax.sharding import PartitionSpec as P

BF = jnp.bfloat16
F32 = jnp.float32
VMEM_LIMIT = 56 * 1024 * 1024
ZN = 4


def params():
    return pltpu.CompilerParams(vmem_limit_bytes=VMEM_LIMIT)


def cost(flops, nbytes):
    return pl.CostEstimate(flops=int(flops), bytes_accessed=int(nbytes), transcendentals=0)


def permuted(value, axis, target):
    return lax.ppermute(value, axis, [(i, target(i)) for i in range(lax.axis_size(axis))])


def mm(a, b, dims):
    return lax.dot_general(a, b, (dims, ((), ())), preferred_element_type=F32)


def columns_of(i, high, width):
    other = high if i < ZN else 1 - high
    return pl.ds(pl.multiple_of(((i % ZN) * 2 + other) * width, width), width)


def dispatch_kernel(high_ref, flat_ref, tok_ref, out_ref):
    tile, features = out_ref.shape
    count = tok_ref.shape[0]
    width = features // (2 * ZN)
    ids = lax.broadcasted_iota(jnp.int32, (tile, count), 0) + pl.program_id(0) * tile
    onehot = (ids == flat_ref[...]).astype(F32).astype(BF)
    for i in range(2 * ZN):
        block = mm(onehot, tok_ref[:, i * width : (i + 1) * width], ((1,), (0,)))
        out_ref[:, columns_of(i, high_ref[0], width)] = block.astype(BF)


def dispatch(high, flat, tok, rows):
    count, features = tok.shape
    tile = min(512, rows)
    return pl.pallas_call(
        dispatch_kernel,
        grid_spec=pltpu.PrefetchScalarGridSpec(
            num_scalar_prefetch=1,
            grid=(rows // tile,),
            in_specs=[
                pl.BlockSpec((1, count), lambda i, high: (0, 0)),
                pl.BlockSpec((count, features), lambda i, high: (0, 0)),
            ],
            out_specs=pl.BlockSpec((tile, features), lambda i, high: (i, 0)),
        ),
        out_shape=jax.ShapeDtypeStruct((rows, features), BF),
        compiler_params=params(),
        cost_estimate=cost(2 * rows * count * features, 2 * features * (rows + count)),
        name="dispatch",
    )(high, flat.reshape(1, count), tok)


def combine_kernel(high_ref, flat_ref, back_ref, out_ref):
    rows, features = back_ref.shape
    width = features // (2 * ZN)
    ids = lax.broadcasted_iota(jnp.int32, (out_ref.shape[0], rows), 1)
    onehot = (ids == flat_ref[...]).astype(F32).astype(BF)
    for i in range(2 * ZN):
        block = mm(onehot, back_ref[:, columns_of(i, high_ref[0], width)], ((1,), (0,)))
        out_ref[:, i * width : (i + 1) * width] = block.astype(BF)


def combine(high, flat, back, count):
    rows, features = back.shape
    tile = min(256, count)
    return pl.pallas_call(
        combine_kernel,
        grid_spec=pltpu.PrefetchScalarGridSpec(
            num_scalar_prefetch=1,
            grid=(count // tile,),
            in_specs=[
                pl.BlockSpec((tile, 1), lambda i, high: (i, 0)),
                pl.BlockSpec((rows, features), lambda i, high: (0, 0)),
            ],
            out_specs=pl.BlockSpec((tile, features), lambda i, high: (i, 0)),
        ),
        out_shape=jax.ShapeDtypeStruct((count, features), BF),
        compiler_params=params(),
        cost_estimate=cost(2 * rows * count * features, 2 * features * (rows + count)),
        name="combine",
    )(high, flat.reshape(count, 1), back)


def forward_kernel(x_ref, gate_ref, up_ref, h_ref, p_ref, s_ref):
    x = x_ref[...]
    g = mm(x, gate_ref[...], ((1,), (0,)))
    u = mm(x, up_ref[...], ((1,), (0,)))
    sig = jax.nn.sigmoid(g)
    s = g * sig
    h_ref[...] = (s * u).astype(BF)
    p_ref[...] = u * sig * (1.0 + g * (1.0 - sig))
    s_ref[...] = s


def forward(x, gate_up):
    rows, features = x.shape
    hidden = gate_up.shape[1] // 2
    tile = min(256, hidden)
    tiles = hidden // tile
    out = pl.BlockSpec((rows, tile), lambda j: (0, j))
    return pl.pallas_call(
        forward_kernel,
        grid=(hidden // tile,),
        in_specs=[
            pl.BlockSpec((rows, features), lambda j: (0, 0)),
            pl.BlockSpec((features, tile), lambda j: (0, j)),
            pl.BlockSpec((features, tile), lambda j: (0, j + tiles)),
        ],
        out_specs=[out, out, out],
        out_shape=[
            jax.ShapeDtypeStruct((rows, hidden), BF),
            jax.ShapeDtypeStruct((rows, hidden), F32),
            jax.ShapeDtypeStruct((rows, hidden), F32),
        ],
        compiler_params=params(),
        cost_estimate=cost(4 * rows * features * hidden, 20e6),
        name="forward",
    )(x, gate_up, gate_up)


def hidden_kernel(z_ref, dy_ref, own_ref, next_ref, last_ref, top_ref, low_ref, p_ref, s_ref, dg_ref, du_ref):
    size = own_ref.shape[0]
    half = size // 2

    def part(away, start, ref):
        block = lax.rem(z_ref[0] + away, ZN)
        columns = pl.ds(pl.multiple_of(block * size + start, half), ref.shape[0])
        return mm(dy_ref[:, columns], ref[...], ((1,), (0,)))

    dh = part(0, 0, own_ref) + part(1, 0, next_ref) + part(ZN - 1, 0, last_ref)
    dh = dh + part(2, 0, top_ref) + part(2, half, low_ref)
    dg_ref[...] = (dh * p_ref[...]).astype(BF)
    du_ref[...] = (dh * s_ref[...]).astype(BF)


def hidden_grads(z, dy, down, p, s):
    rows, features = dy.shape
    hidden = p.shape[1]
    tile = min(256, rows)
    out = pl.BlockSpec((tile, hidden), lambda i, z: (i, 0))
    return pl.pallas_call(
        hidden_kernel,
        grid_spec=pltpu.PrefetchScalarGridSpec(
            num_scalar_prefetch=1,
            grid=(rows // tile,),
            in_specs=[pl.BlockSpec((tile, features), lambda i, z: (i, 0))]
            + [pl.BlockSpec(v.shape, lambda i, z: (0, 0)) for v in down]
            + [out, out],
            out_specs=[out, out],
        ),
        out_shape=[jax.ShapeDtypeStruct((rows, hidden), BF)] * 2,
        compiler_params=params(),
        cost_estimate=cost(2 * rows * features * hidden, 17e6),
        name="hidden_grads",
    )(z, dy, *down, p, s)


def weight_kernel(shift_ref, a_ref, b_ref, out_ref):
    out_ref[...] = mm(a_ref[...], b_ref[...], ((0,), (0,))).astype(BF)


def weight_grad(shift, a, b, name):
    rows, features = a.shape
    hidden = b.shape[1]
    tile = features // ZN
    return pl.pallas_call(
        weight_kernel,
        grid_spec=pltpu.PrefetchScalarGridSpec(
            num_scalar_prefetch=1,
            grid=(ZN,),
            in_specs=[
                pl.BlockSpec((rows, tile), lambda i, shift: (0, (i + shift[0]) % ZN)),
                pl.BlockSpec((rows, hidden), lambda i, shift: (0, 0)),
            ],
            out_specs=pl.BlockSpec((tile, hidden), lambda i, shift: (i, 0)),
        ),
        out_shape=jax.ShapeDtypeStruct((features, hidden), BF),
        compiler_params=params(),
        cost_estimate=cost(2 * rows * features * hidden, 9e6),
        name=name,
    )(shift, a, b)


def input_kernel(dg_ref, du_ref, gate_ref, up_ref, out_ref):
    acc = mm(dg_ref[...], gate_ref[...], ((1,), (1,)))
    acc = acc + mm(du_ref[...], up_ref[...], ((1,), (1,)))
    out_ref[...] = acc.astype(BF)


def input_grad(dg, du, gate_up):
    rows, hidden = dg.shape
    features = gate_up.shape[0]
    tile = 512
    left = pl.BlockSpec((rows, hidden), lambda i: (0, 0))
    gate = pl.BlockSpec((tile, hidden), lambda i: (i, 0))
    up = pl.BlockSpec((tile, hidden), lambda i: (i, 1))
    return pl.pallas_call(
        input_kernel,
        grid=(features // tile,),
        in_specs=[left, left, gate, up],
        out_specs=pl.BlockSpec((rows, tile), lambda i: (0, i)),
        out_shape=jax.ShapeDtypeStruct((rows, features), BF),
        compiler_params=params(),
        cost_estimate=cost(4 * rows * features * hidden, 14e6),
        name="input_grad",
    )(dg, du, gate_up, gate_up)


def adam_kernel(n_sums, keep_ref, *refs):
    w_ref, m_ref, v_ref, wb_ref, mb_ref, vb_ref = refs[n_sums : n_sums + 6]
    nw_ref, nm_ref, nv_ref = refs[-3:]
    keep = keep_ref[0] != 0
    grad = sum(ref[...].astype(F32) for ref in refs[:n_sums])
    w = jnp.where(keep, w_ref[...], wb_ref[...].astype(F32))
    m = jnp.where(keep, m_ref[...], mb_ref[...].astype(F32))
    v = jnp.where(keep, v_ref[...], vb_ref[...].astype(F32))
    m = 0.9 * m + 0.1 * grad
    v = 0.95 * v + 0.05 * grad * grad
    update = m / (1.0 - 0.9**10) / (jnp.sqrt(v / (1.0 - 0.95**10)) + 1e-08)
    nw_ref[...] = w - 0.003 * (update + 0.1 * w)
    nm_ref[...] = m
    nv_ref[...] = v


def adam(keep, sums, state, moved, k, before):
    rows, hidden = sums[0].shape
    tile = min(128, rows)
    chunk = pl.BlockSpec((tile, hidden), lambda i, keep: (i, 0))
    column = pl.BlockSpec((tile, hidden), lambda i, keep: (i, k))
    shape = jax.ShapeDtypeStruct(state[0].shape, F32)

    def at(block):
        return pl.BlockSpec((tile, hidden), lambda i, keep: (i, block))

    return pl.pallas_call(
        functools.partial(adam_kernel, len(sums)),
        grid_spec=pltpu.PrefetchScalarGridSpec(
            num_scalar_prefetch=1,
            grid=(rows // tile,),
            in_specs=[chunk] * len(sums)
            + [column] * 3
            + [at(block) for _, block in moved]
            + [pl.BlockSpec(memory_space=pl.ANY)] * len(before),
            out_specs=[column] * 3,
        ),
        out_shape=[shape] * 3,
        input_output_aliases={len(sums) + 7 + i: i for i in range(len(before))},
        compiler_params=params(),
        cost_estimate=cost(20 * rows * hidden, 34 * rows * hidden),
        name="adam",
    )(keep, *sums, *state, *[v for v, _ in moved], *before)


def per_device(tokens, cotangent, routes, owner, master, moment1, moment2):
    experts = lax.axis_size("expert")
    half = experts // 2
    position = lax.axis_index("expert")
    high = (lax.axis_index("dp") // ZN).astype(jnp.int32).reshape(1)
    keep = owner[position] == position
    info = keep.astype(jnp.int32).reshape(1)
    hidden = master.shape[2] // 3
    features = tokens.shape[2]
    count = tokens.shape[1]
    capacity = 2 * count // experts
    rows = experts * capacity
    replicas = lax.axis_size("dp")
    z_groups = [[h * ZN + z for z in range(ZN)] for h in range(replicas // ZN)]

    route_ids = routes[0, :, 0]
    columns = jnp.arange(experts, dtype=jnp.int32)
    onehot = (route_ids[:, None] == columns[None, :]).astype(jnp.int32)
    slot = jnp.sum((jnp.cumsum(onehot, axis=0) - 1) * onehot, axis=1)
    flat = route_ids * capacity + slot
    send_x = dispatch(high, flat, tokens[0], rows)
    send_dy = dispatch(high, flat, cotangent[0], rows)

    def over_owners(value):
        return permuted(value, "expert", lambda i: i ^ half)

    def over_high(value):
        return permuted(value, "dp", lambda i: i ^ ZN)

    def over_experts(value):
        boxes = value.reshape(experts, capacity, value.shape[1])
        out = lax.all_to_all(boxes, "expert", split_axis=0, concat_axis=0, tiled=True)
        return out.reshape(value.shape)

    def gathered(value):
        return lax.all_gather(value, "dp", axis=0, tiled=True, axis_index_groups=z_groups)

    def scattered(grad):
        return lax.psum_scatter(
            grad, "dp", scatter_dimension=0, tiled=True, axis_index_groups=z_groups
        )

    def to_next(value):
        return permuted(value, "dp", lambda i: i // ZN * ZN + (i + 1) % ZN)

    def to_last(value):
        return permuted(value, "dp", lambda i: i // ZN * ZN + (i - 1) % ZN)

    z = (lax.axis_index("dp") % ZN).astype(jnp.int32).reshape(1)
    nought = jnp.zeros((1,), jnp.int32)

    split = 2 * hidden
    own_a, own_b = master[0, :, :split].astype(BF), master[0, :, split:].astype(BF)
    other_a = over_owners(own_a)
    own_b, other_a = lax.optimization_barrier((own_b, other_a))
    other_b = over_owners(own_b)
    placed_a = lax.optimization_barrier(jnp.where(keep, own_a, other_a))
    far_a = over_high(placed_a)
    placed_a, far_a, other_b, send_x = lax.optimization_barrier((placed_a, far_a, other_b, send_x))
    gate_up = gathered(jnp.concatenate([placed_a, far_a], axis=0))
    x = over_experts(send_x)
    placed_b = jnp.where(keep, own_b, other_b)
    far_b = over_high(placed_b)
    down_own = jnp.concatenate([placed_b, far_b], axis=0)
    send_dy, x, down_own = lax.optimization_barrier((send_dy, x, down_own))
    dy = over_experts(send_dy)
    down_last, down_next = to_next(down_own), to_last(down_own)
    h, p, s = forward(x, gate_up)
    down_last, down_next, h = lax.optimization_barrier((down_last, down_next, h))
    quarter = down_own.shape[0] // 2
    down = (down_own, down_next, down_last, to_next(down_last[:quarter]), to_last(down_next[quarter:]))

    def ring_first(grad):
        return to_next(grad[2, 0]), to_last(grad[2, 1])

    def ring_second(grad, top, low):
        top = (grad[1, 0].astype(F32) + top.astype(F32)).astype(BF)
        low = (grad[ZN - 1, 1].astype(F32) + low.astype(F32)).astype(BF)
        return to_next(jnp.stack([top, grad[1, 1]])), to_last(jnp.stack([grad[ZN - 1, 0], low]))

    def ring_sum(grad, ahead, behind):
        part = grad[0].astype(F32) + ahead.astype(F32) + behind.astype(F32)
        return part.astype(BF)

    def blocks(grad):
        return grad.reshape(ZN, 2, -1, hidden)

    together = lax.optimization_barrier

    m_all, v_all = moment1[0].astype(BF), moment2[0].astype(BF)
    m_own = jnp.concatenate([m_all[:, :hidden], m_all[:, split:]], axis=1)
    v_own = [v_all[:, split:], v_all[:, :hidden]]
    v_own.append(jnp.concatenate([m_all[:, hidden:split], v_all[:, hidden:split]], axis=1))
    dy, m_own, *others = together((dy, m_own, *v_own, *down[3:]))
    v_own, down = others[:3], (*down[:3], *others[3:])
    part_down = scattered(weight_grad(nought, dy, h, "grad_down")).reshape(2, -1, hidden)
    m_other = over_owners(m_own)
    dg, du = hidden_grads(z, dy, down, p, s)
    send_back = input_grad(dg, du, gate_up)
    send_back, m_other, dg, du = together((send_back, m_other, dg, du))
    returned = over_experts(send_back)

    gate = blocks(weight_grad(z, x, dg, "grad_gate"))
    gate, du = together((gate, du))
    first = ring_first(gate)
    up = blocks(weight_grad(z, x, du, "grad_up"))
    first, up, *v_own = together((first, up, *v_own))
    second = ring_second(gate, *first)
    first = ring_first(up)
    first, second, part_down = together((first, second, part_down))
    part_gate = ring_sum(gate, *second)
    far_gate, far_down = over_high(part_gate[1]), over_high(part_down[1])
    v_other = [over_owners(v) for v in v_own]
    second = ring_second(up, *first)
    second, v_other[0] = together((second, v_other[0]))
    part_up = ring_sum(up, *second)
    far_up = over_high(part_up[1])
    token_grad = combine(high, flat, returned, count)

    state = (master[0], moment1[0], moment2[0])
    steps = (
        (2, part_down[0], far_down, ((other_b, 0), (m_other, 1), (v_other[0], 0))),
        (0, part_gate[0], far_gate, ((other_a, 0), (m_other, 0), (v_other[1], 0))),
        (1, part_up[0], far_up, ((other_a, 1), (v_other[2], 0), (v_other[2], 1))),
    )
    new = ()
    for k, near, far, moved in steps:
        new = adam(info, (near, far), state, moved, k, new)
    return (token_grad[None], new[0][None], new[1][None], new[2][None])


def solution(mesh):
    placed = (
        P("dp", "expert", None),
        P("dp", "expert", None),
        P("dp", "expert", None),
        P(),
        P("expert", "dp", None),
        P("expert", "dp", None),
        P("expert", "dp", None),
    )
    return jax.shard_map(
        per_device,
        mesh=mesh,
        in_specs=placed,
        out_specs=(
            P("dp", "expert", None),
            P("expert", "dp", None),
            P("expert", "dp", None),
            P("expert", "dp", None),
        ),
        check_vma=False,
    )
```

```python
import functools
import jax
import jax.numpy as jnp
from jax import lax
from jax.experimental import pallas as pl
from jax.experimental.pallas import tpu as pltpu
from jax.sharding import PartitionSpec as P

BF = jnp.bfloat16
F32 = jnp.float32
VMEM_LIMIT = 56 * 1024 * 1024
ZN = 4


def params():
    return pltpu.CompilerParams(vmem_limit_bytes=VMEM_LIMIT)


def cost(flops, nbytes):
    return pl.CostEstimate(flops=int(flops), bytes_accessed=int(nbytes), transcendentals=0)


def permuted(value, axis, target):
    return lax.ppermute(value, axis, [(i, target(i)) for i in range(lax.axis_size(axis))])


def mm(a, b, dims):
    return lax.dot_general(a, b, (dims, ((), ())), preferred_element_type=F32)


def columns_of(i, high, width):
    other = high if i < ZN else 1 - high
    return pl.ds(pl.multiple_of(((i % ZN) * 2 + other) * width, width), width)


def dispatch_kernel(high_ref, flat_ref, tok_ref, out_ref):
    tile, features = out_ref.shape
    count = tok_ref.shape[0]
    width = features // (2 * ZN)
    ids = lax.broadcasted_iota(jnp.int32, (tile, count), 0) + pl.program_id(0) * tile
    onehot = (ids == flat_ref[...]).astype(F32).astype(BF)
    for i in range(2 * ZN):
        block = mm(onehot, tok_ref[:, i * width : (i + 1) * width], ((1,), (0,)))
        out_ref[:, columns_of(i, high_ref[0], width)] = block.astype(BF)


def dispatch(high, flat, tok, rows):
    count, features = tok.shape
    tile = min(512, rows)
    return pl.pallas_call(
        dispatch_kernel,
        grid_spec=pltpu.PrefetchScalarGridSpec(
            num_scalar_prefetch=1,
            grid=(rows // tile,),
            in_specs=[
                pl.BlockSpec((1, count), lambda i, high: (0, 0)),
                pl.BlockSpec((count, features), lambda i, high: (0, 0)),
            ],
            out_specs=pl.BlockSpec((tile, features), lambda i, high: (i, 0)),
        ),
        out_shape=jax.ShapeDtypeStruct((rows, features), BF),
        compiler_params=params(),
        cost_estimate=cost(2 * rows * count * features, 2 * features * (rows + count)),
        name="dispatch",
    )(high, flat.reshape(1, count), tok)


def combine_kernel(high_ref, flat_ref, back_ref, out_ref):
    rows, features = back_ref.shape
    width = features // (2 * ZN)
    ids = lax.broadcasted_iota(jnp.int32, (out_ref.shape[0], rows), 1)
    onehot = (ids == flat_ref[...]).astype(F32).astype(BF)
    for i in range(2 * ZN):
        block = mm(onehot, back_ref[:, columns_of(i, high_ref[0], width)], ((1,), (0,)))
        out_ref[:, i * width : (i + 1) * width] = block.astype(BF)


def combine(high, flat, back, count):
    rows, features = back.shape
    tile = min(256, count)
    return pl.pallas_call(
        combine_kernel,
        grid_spec=pltpu.PrefetchScalarGridSpec(
            num_scalar_prefetch=1,
            grid=(count // tile,),
            in_specs=[
                pl.BlockSpec((tile, 1), lambda i, high: (i, 0)),
                pl.BlockSpec((rows, features), lambda i, high: (0, 0)),
            ],
            out_specs=pl.BlockSpec((tile, features), lambda i, high: (i, 0)),
        ),
        out_shape=jax.ShapeDtypeStruct((count, features), BF),
        compiler_params=params(),
        cost_estimate=cost(2 * rows * count * features, 2 * features * (rows + count)),
        name="combine",
    )(high, flat.reshape(count, 1), back)


def forward_kernel(x_ref, gate_ref, up_ref, h_ref, p_ref, s_ref):
    x = x_ref[...]
    g = mm(x, gate_ref[...], ((1,), (0,)))
    u = mm(x, up_ref[...], ((1,), (0,)))
    sig = jax.nn.sigmoid(g)
    s = g * sig
    h_ref[...] = (s * u).astype(BF)
    p_ref[...] = u * sig * (1.0 + g * (1.0 - sig))
    s_ref[...] = s


def forward(x, gate_up):
    rows, features = x.shape
    hidden = gate_up.shape[1] // 2
    tile = min(256, hidden)
    tiles = hidden // tile
    out = pl.BlockSpec((rows, tile), lambda j: (0, j))
    return pl.pallas_call(
        forward_kernel,
        grid=(hidden // tile,),
        in_specs=[
            pl.BlockSpec((rows, features), lambda j: (0, 0)),
            pl.BlockSpec((features, tile), lambda j: (0, j)),
            pl.BlockSpec((features, tile), lambda j: (0, j + tiles)),
        ],
        out_specs=[out, out, out],
        out_shape=[
            jax.ShapeDtypeStruct((rows, hidden), BF),
            jax.ShapeDtypeStruct((rows, hidden), F32),
            jax.ShapeDtypeStruct((rows, hidden), F32),
        ],
        compiler_params=params(),
        cost_estimate=cost(4 * rows * features * hidden, 20e6),
        name="forward",
    )(x, gate_up, gate_up)


def hidden_kernel(z_ref, dy_ref, own_ref, next_ref, last_ref, top_ref, low_ref, p_ref, s_ref, dg_ref, du_ref):
    size = own_ref.shape[0]
    half = size // 2

    def part(away, start, ref):
        block = lax.rem(z_ref[0] + away, ZN)
        columns = pl.ds(pl.multiple_of(block * size + start, half), ref.shape[0])
        return mm(dy_ref[:, columns], ref[...], ((1,), (0,)))

    dh = part(0, 0, own_ref) + part(1, 0, next_ref) + part(ZN - 1, 0, last_ref)
    dh = dh + part(2, 0, top_ref) + part(2, half, low_ref)
    dg_ref[...] = (dh * p_ref[...]).astype(BF)
    du_ref[...] = (dh * s_ref[...]).astype(BF)


def hidden_grads(z, dy, down, p, s):
    rows, features = dy.shape
    hidden = p.shape[1]
    tile = min(256, rows)
    out = pl.BlockSpec((tile, hidden), lambda i, z: (i, 0))
    return pl.pallas_call(
        hidden_kernel,
        grid_spec=pltpu.PrefetchScalarGridSpec(
            num_scalar_prefetch=1,
            grid=(rows // tile,),
            in_specs=[pl.BlockSpec((tile, features), lambda i, z: (i, 0))]
            + [pl.BlockSpec(v.shape, lambda i, z: (0, 0)) for v in down]
            + [out, out],
            out_specs=[out, out],
        ),
        out_shape=[jax.ShapeDtypeStruct((rows, hidden), BF)] * 2,
        compiler_params=params(),
        cost_estimate=cost(2 * rows * features * hidden, 17e6),
        name="hidden_grads",
    )(z, dy, *down, p, s)


def weight_kernel(shift_ref, a_ref, b_ref, out_ref):
    out_ref[...] = mm(a_ref[...], b_ref[...], ((0,), (0,))).astype(BF)


def weight_grad(shift, a, b, name):
    rows, features = a.shape
    hidden = b.shape[1]
    tile = features // ZN
    return pl.pallas_call(
        weight_kernel,
        grid_spec=pltpu.PrefetchScalarGridSpec(
            num_scalar_prefetch=1,
            grid=(ZN,),
            in_specs=[
                pl.BlockSpec((rows, tile), lambda i, shift: (0, (i + shift[0]) % ZN)),
                pl.BlockSpec((rows, hidden), lambda i, shift: (0, 0)),
            ],
            out_specs=pl.BlockSpec((tile, hidden), lambda i, shift: (i, 0)),
        ),
        out_shape=jax.ShapeDtypeStruct((features, hidden), BF),
        compiler_params=params(),
        cost_estimate=cost(2 * rows * features * hidden, 9e6),
        name=name,
    )(shift, a, b)


def ring_kernel(block_ref, first_ref, second_ref, b_ref, *out_refs):
    half = first_ref.shape[1]
    top = mm(first_ref[...], b_ref[...], ((0,), (0,))).astype(BF)
    low = mm(second_ref[...], b_ref[...], ((0,), (0,))).astype(BF)
    for k, out_ref in enumerate(out_refs):

        @pl.when(pl.program_id(0) == k)
        def _():
            out_ref[:half, :] = top
            out_ref[half:, :] = low


RING_PARTS = (((2, 0), (1, 1)), ((2, 1), (3, 0)), ((1, 0), (3, 1)), ((0, 0), (0, 1)))


def ring_grad(z, a, b, name):
    rows, features = a.shape
    hidden = b.shape[1]
    width = features // (2 * ZN)
    blocks = [(z + far) % ZN * 2 + r for pair in RING_PARTS for far, r in pair]
    part = pl.BlockSpec((2 * width, hidden), lambda i, blocks: (0, 0))
    return pl.pallas_call(
        ring_kernel,
        grid_spec=pltpu.PrefetchScalarGridSpec(
            num_scalar_prefetch=1,
            grid=(ZN,),
            in_specs=[
                pl.BlockSpec((rows, width), lambda i, blocks: (0, blocks[2 * i])),
                pl.BlockSpec((rows, width), lambda i, blocks: (0, blocks[2 * i + 1])),
                pl.BlockSpec((rows, hidden), lambda i, blocks: (0, 0)),
            ],
            out_specs=[part] * ZN,
        ),
        out_shape=[jax.ShapeDtypeStruct((2 * width, hidden), BF)] * ZN,
        compiler_params=params(),
        cost_estimate=cost(2 * rows * features * hidden, 9e6),
        name=name,
    )(jnp.concatenate(blocks), a, a, b)


def input_kernel(dg_ref, du_ref, gate_ref, up_ref, out_ref):
    acc = mm(dg_ref[...], gate_ref[...], ((1,), (1,)))
    acc = acc + mm(du_ref[...], up_ref[...], ((1,), (1,)))
    out_ref[...] = acc.astype(BF)


def input_grad(dg, du, gate_up):
    rows, hidden = dg.shape
    features = gate_up.shape[0]
    tile = 512
    left = pl.BlockSpec((rows, hidden), lambda i: (0, 0))
    gate = pl.BlockSpec((tile, hidden), lambda i: (i, 0))
    up = pl.BlockSpec((tile, hidden), lambda i: (i, 1))
    return pl.pallas_call(
        input_kernel,
        grid=(features // tile,),
        in_specs=[left, left, gate, up],
        out_specs=pl.BlockSpec((rows, tile), lambda i: (0, i)),
        out_shape=jax.ShapeDtypeStruct((rows, features), BF),
        compiler_params=params(),
        cost_estimate=cost(4 * rows * features * hidden, 14e6),
        name="input_grad",
    )(dg, du, gate_up, gate_up)


def adam_kernel(n_sums, keep_ref, *refs):
    w_ref, m_ref, v_ref, wb_ref, mb_ref, vb_ref = refs[n_sums : n_sums + 6]
    nw_ref, nm_ref, nv_ref = refs[-3:]
    keep = keep_ref[0] != 0
    grad = sum(ref[...].astype(F32) for ref in refs[:n_sums])
    w = jnp.where(keep, w_ref[...], wb_ref[...].astype(F32))
    m = jnp.where(keep, m_ref[...], mb_ref[...].astype(F32))
    v = jnp.where(keep, v_ref[...], vb_ref[...].astype(F32))
    m = 0.9 * m + 0.1 * grad
    v = 0.95 * v + 0.05 * grad * grad
    update = m / (1.0 - 0.9**10) / (jnp.sqrt(v / (1.0 - 0.95**10)) + 1e-08)
    nw_ref[...] = w - 0.003 * (update + 0.1 * w)
    nm_ref[...] = m
    nv_ref[...] = v


def adam(keep, sums, state, moved, k, before):
    rows, hidden = state[0].shape[0], sums[0][0].shape[1]
    tile = min(128, rows)
    steps = rows // tile
    column = pl.BlockSpec((tile, hidden), lambda i, keep: (i, k))
    shape = jax.ShapeDtypeStruct(state[0].shape, F32)

    def at(block):
        return pl.BlockSpec((tile, hidden), lambda i, keep: (i, block))

    def term(half):
        return pl.BlockSpec((tile, hidden), lambda i, keep: (i + half * steps, 0))

    return pl.pallas_call(
        functools.partial(adam_kernel, len(sums)),
        grid_spec=pltpu.PrefetchScalarGridSpec(
            num_scalar_prefetch=1,
            grid=(steps,),
            in_specs=[term(half) for _, half in sums]
            + [column] * 3
            + [at(block) for _, block in moved]
            + [pl.BlockSpec(memory_space=pl.ANY)] * len(before),
            out_specs=[column] * 3,
        ),
        out_shape=[shape] * 3,
        input_output_aliases={len(sums) + 7 + i: i for i in range(len(before))},
        compiler_params=params(),
        cost_estimate=cost(20 * rows * hidden, 34 * rows * hidden),
        name="adam",
    )(keep, *[v for v, _ in sums], *state, *[v for v, _ in moved], *before)


def per_device(tokens, cotangent, routes, owner, master, moment1, moment2):
    experts = lax.axis_size("expert")
    half = experts // 2
    position = lax.axis_index("expert")
    high = (lax.axis_index("dp") // ZN).astype(jnp.int32).reshape(1)
    keep = owner[position] == position
    info = keep.astype(jnp.int32).reshape(1)
    hidden = master.shape[2] // 3
    features = tokens.shape[2]
    count = tokens.shape[1]
    capacity = 2 * count // experts
    rows = experts * capacity
    replicas = lax.axis_size("dp")
    z_groups = [[h * ZN + z for z in range(ZN)] for h in range(replicas // ZN)]

    route_ids = routes[0, :, 0]
    columns = jnp.arange(experts, dtype=jnp.int32)
    onehot = (route_ids[:, None] == columns[None, :]).astype(jnp.int32)
    slot = jnp.sum((jnp.cumsum(onehot, axis=0) - 1) * onehot, axis=1)
    flat = route_ids * capacity + slot
    send_x = dispatch(high, flat, tokens[0], rows)
    send_dy = dispatch(high, flat, cotangent[0], rows)

    def over_owners(value):
        return permuted(value, "expert", lambda i: i ^ half)

    def over_high(value):
        return permuted(value, "dp", lambda i: i ^ ZN)

    def over_experts(value):
        boxes = value.reshape(experts, capacity, value.shape[1])
        out = lax.all_to_all(boxes, "expert", split_axis=0, concat_axis=0, tiled=True)
        return out.reshape(value.shape)

    def gathered(value):
        return lax.all_gather(value, "dp", axis=0, tiled=True, axis_index_groups=z_groups)

    def scattered(grad):
        return lax.psum_scatter(
            grad, "dp", scatter_dimension=0, tiled=True, axis_index_groups=z_groups
        )

    def to_next(value):
        return permuted(value, "dp", lambda i: i // ZN * ZN + (i + 1) % ZN)

    def to_last(value):
        return permuted(value, "dp", lambda i: i // ZN * ZN + (i - 1) % ZN)

    z = (lax.axis_index("dp") % ZN).astype(jnp.int32).reshape(1)
    nought = jnp.zeros((1,), jnp.int32)

    split = 2 * hidden
    own_a, own_b = master[0, :, :split].astype(BF), master[0, :, split:].astype(BF)
    other_a = over_owners(own_a)
    own_b, other_a = lax.optimization_barrier((own_b, other_a))
    other_b = over_owners(own_b)
    placed_a = lax.optimization_barrier(jnp.where(keep, own_a, other_a))
    far_a = over_high(placed_a)
    placed_a, far_a, other_b, send_x = lax.optimization_barrier((placed_a, far_a, other_b, send_x))
    gate_up = gathered(jnp.concatenate([placed_a, far_a], axis=0))
    x = over_experts(send_x)
    placed_b = jnp.where(keep, own_b, other_b)
    far_b = over_high(placed_b)
    down_own = jnp.concatenate([placed_b, far_b], axis=0)
    send_dy, x, down_own = lax.optimization_barrier((send_dy, x, down_own))
    dy = over_experts(send_dy)
    down_last, down_next = to_next(down_own), to_last(down_own)
    h, p, s = forward(x, gate_up)
    down_last, down_next, h = lax.optimization_barrier((down_last, down_next, h))
    quarter = down_own.shape[0] // 2
    down = (down_own, down_next, down_last, to_next(down_last[:quarter]), to_last(down_next[quarter:]))

    def ring_first(parts):
        return to_next(parts[0]), to_last(parts[1])

    def ring_second(parts, ahead, behind):
        size = ahead.shape[0] // 2
        top = parts[2][:size].astype(F32) + ahead[:size].astype(F32)
        low = parts[2][size:].astype(F32) + behind[:size].astype(F32)
        return to_next(top.astype(BF)), to_last(low.astype(BF))

    def ring_away(parts, ahead, behind, top, low):
        size = top.shape[0]
        away = parts[3][size:].astype(F32) + low.astype(F32) + ahead[size:].astype(F32)
        return away.astype(BF)

    def ring_near(parts, ahead, behind, top, low):
        return (parts[3], 0), (top, 0), (behind, 1)

    together = lax.optimization_barrier

    m_all, v_all = moment1[0].astype(BF), moment2[0].astype(BF)
    m_own = jnp.concatenate([m_all[:, :hidden], m_all[:, split:]], axis=1)
    v_own = [
        jnp.concatenate([v_all[:, split:], v_all[:, :hidden]], axis=1),
        jnp.concatenate([m_all[:, hidden:split], v_all[:, hidden:split]], axis=1),
    ]
    dy, m_own, *others = together((dy, m_own, *v_own, *down[3:]))
    v_own, down = others[:2], (*down[:3], *others[2:])
    part_down = scattered(weight_grad(nought, dy, h, "grad_down")).reshape(2, -1, hidden)
    m_other = over_owners(m_own)
    dg, du = hidden_grads(z, dy, down, p, s)
    send_back = input_grad(dg, du, gate_up)
    send_back, m_other, dg, du = together((send_back, m_other, dg, du))
    returned = over_experts(send_back)

    gate = ring_grad(z, x, dg, "grad_gate")
    gate, du = together((gate, du))
    first_gate = ring_first(gate)
    up = ring_grad(z, x, du, "grad_up")
    first_up = ring_first(up)
    first_gate, up, v_own = together((first_gate, up, v_own))
    second_gate = ring_second(gate, *first_gate)
    far_down = over_high(part_down[1])
    token_grad = combine(high, flat, returned, count)
    first_up, second_gate, far_down, token_grad = together(
        (first_up, second_gate, far_down, token_grad)
    )
    far_gate = over_high(ring_away(gate, *first_gate, *second_gate))
    v_other = [over_owners(v) for v in v_own]
    second_up = ring_second(up, *first_up)
    second_up, v_other[0] = together((second_up, v_other[0]))
    far_up = over_high(ring_away(up, *first_up, *second_up))

    state = (master[0], moment1[0], moment2[0])
    steps = (
        (2, ((part_down[0], 0), (far_down, 0)), ((other_b, 0), (m_other, 1), (v_other[0], 0))),
        (
            0,
            (*ring_near(gate, *first_gate, *second_gate), (far_gate, 0)),
            ((other_a, 0), (m_other, 0), (v_other[0], 1)),
        ),
        (
            1,
            (*ring_near(up, *first_up, *second_up), (far_up, 0)),
            ((other_a, 1), (v_other[1], 0), (v_other[1], 1)),
        ),
    )
    new = ()
    for k, sums, moved in steps:
        new = adam(info, sums, state, moved, k, new)
    return (token_grad[None], new[0][None], new[1][None], new[2][None])


def solution(mesh):
    placed = (
        P("dp", "expert", None),
        P("dp", "expert", None),
        P("dp", "expert", None),
        P(),
        P("expert", "dp", None),
        P("expert", "dp", None),
        P("expert", "dp", None),
    )
    return jax.shard_map(
        per_device,
        mesh=mesh,
        in_specs=placed,
        out_specs=(
            P("dp", "expert", None),
            P("expert", "dp", None),
            P("expert", "dp", None),
            P("expert", "dp", None),
        ),
        check_vma=False,
    )
```

```python
import functools
import jax
import jax.numpy as jnp
from jax import lax
from jax.experimental import pallas as pl
from jax.experimental.pallas import tpu as pltpu
from jax.sharding import PartitionSpec as P

BF = jnp.bfloat16
F32 = jnp.float32
VMEM_LIMIT = 56 * 1024 * 1024
ZN = 4


def params():
    return pltpu.CompilerParams(vmem_limit_bytes=VMEM_LIMIT)


def cost(flops, nbytes):
    return pl.CostEstimate(flops=int(flops), bytes_accessed=int(nbytes), transcendentals=0)


def permuted(value, axis, target):
    return lax.ppermute(value, axis, [(i, target(i)) for i in range(lax.axis_size(axis))])


def mm(a, b, dims):
    return lax.dot_general(a, b, (dims, ((), ())), preferred_element_type=F32)


def columns_of(i, high, width):
    other = high if i < ZN else 1 - high
    return pl.ds(pl.multiple_of(((i % ZN) * 2 + other) * width, width), width)


def dispatch_kernel(high_ref, flat_ref, tok_ref, out_ref):
    tile, features = out_ref.shape
    count = tok_ref.shape[0]
    width = features // (2 * ZN)
    ids = lax.broadcasted_iota(jnp.int32, (tile, count), 0) + pl.program_id(0) * tile
    onehot = (ids == flat_ref[...]).astype(F32).astype(BF)
    for i in range(2 * ZN):
        block = mm(onehot, tok_ref[:, i * width : (i + 1) * width], ((1,), (0,)))
        out_ref[:, columns_of(i, high_ref[0], width)] = block.astype(BF)


def dispatch(high, flat, tok, rows):
    count, features = tok.shape
    tile = min(512, rows)
    return pl.pallas_call(
        dispatch_kernel,
        grid_spec=pltpu.PrefetchScalarGridSpec(
            num_scalar_prefetch=1,
            grid=(rows // tile,),
            in_specs=[
                pl.BlockSpec((1, count), lambda i, high: (0, 0)),
                pl.BlockSpec((count, features), lambda i, high: (0, 0)),
            ],
            out_specs=pl.BlockSpec((tile, features), lambda i, high: (i, 0)),
        ),
        out_shape=jax.ShapeDtypeStruct((rows, features), BF),
        compiler_params=params(),
        cost_estimate=cost(2 * rows * count * features, 2 * features * (rows + count)),
        name="dispatch",
    )(high, flat.reshape(1, count), tok)


def combine_kernel(high_ref, flat_ref, back_ref, out_ref):
    rows, features = back_ref.shape
    width = features // (2 * ZN)
    ids = lax.broadcasted_iota(jnp.int32, (out_ref.shape[0], rows), 1)
    onehot = (ids == flat_ref[...]).astype(F32).astype(BF)
    for i in range(2 * ZN):
        block = mm(onehot, back_ref[:, columns_of(i, high_ref[0], width)], ((1,), (0,)))
        out_ref[:, i * width : (i + 1) * width] = block.astype(BF)


def combine(high, flat, back, count):
    rows, features = back.shape
    tile = min(256, count)
    return pl.pallas_call(
        combine_kernel,
        grid_spec=pltpu.PrefetchScalarGridSpec(
            num_scalar_prefetch=1,
            grid=(count // tile,),
            in_specs=[
                pl.BlockSpec((tile, 1), lambda i, high: (i, 0)),
                pl.BlockSpec((rows, features), lambda i, high: (0, 0)),
            ],
            out_specs=pl.BlockSpec((tile, features), lambda i, high: (i, 0)),
        ),
        out_shape=jax.ShapeDtypeStruct((count, features), BF),
        compiler_params=params(),
        cost_estimate=cost(2 * rows * count * features, 2 * features * (rows + count)),
        name="combine",
    )(high, flat.reshape(count, 1), back)


def forward_kernel(x_ref, gate_ref, up_ref, h_ref, p_ref, s_ref):
    x = x_ref[...]
    g = mm(x, gate_ref[...], ((1,), (0,)))
    u = mm(x, up_ref[...], ((1,), (0,)))
    sig = jax.nn.sigmoid(g)
    s = g * sig
    h_ref[...] = (s * u).astype(BF)
    p_ref[...] = u * sig * (1.0 + g * (1.0 - sig))
    s_ref[...] = s


def forward(x, gate_up):
    rows, features = x.shape
    hidden = gate_up.shape[1] // 2
    tile = min(256, hidden)
    tiles = hidden // tile
    out = pl.BlockSpec((rows, tile), lambda j: (0, j))
    return pl.pallas_call(
        forward_kernel,
        grid=(hidden // tile,),
        in_specs=[
            pl.BlockSpec((rows, features), lambda j: (0, 0)),
            pl.BlockSpec((features, tile), lambda j: (0, j)),
            pl.BlockSpec((features, tile), lambda j: (0, j + tiles)),
        ],
        out_specs=[out, out, out],
        out_shape=[
            jax.ShapeDtypeStruct((rows, hidden), BF),
            jax.ShapeDtypeStruct((rows, hidden), F32),
            jax.ShapeDtypeStruct((rows, hidden), F32),
        ],
        compiler_params=params(),
        cost_estimate=cost(4 * rows * features * hidden, 20e6),
        name="forward",
    )(x, gate_up, gate_up)


def hidden_kernel(z_ref, dy_ref, own_ref, next_ref, last_ref, top_ref, low_ref, p_ref, s_ref, dg_ref, du_ref):
    size = own_ref.shape[0]
    half = size // 2

    def part(away, start, ref):
        block = lax.rem(z_ref[0] + away, ZN)
        columns = pl.ds(pl.multiple_of(block * size + start, half), ref.shape[0])
        return mm(dy_ref[:, columns], ref[...], ((1,), (0,)))

    dh = part(0, 0, own_ref) + part(1, 0, next_ref) + part(ZN - 1, 0, last_ref)
    dh = dh + part(2, 0, top_ref) + part(2, half, low_ref)
    dg_ref[...] = (dh * p_ref[...]).astype(BF)
    du_ref[...] = (dh * s_ref[...]).astype(BF)


def hidden_grads(z, dy, down, p, s):
    rows, features = dy.shape
    hidden = p.shape[1]
    tile = min(256, rows)
    out = pl.BlockSpec((tile, hidden), lambda i, z: (i, 0))
    return pl.pallas_call(
        hidden_kernel,
        grid_spec=pltpu.PrefetchScalarGridSpec(
            num_scalar_prefetch=1,
            grid=(rows // tile,),
            in_specs=[pl.BlockSpec((tile, features), lambda i, z: (i, 0))]
            + [pl.BlockSpec(v.shape, lambda i, z: (0, 0)) for v in down]
            + [out, out],
            out_specs=[out, out],
        ),
        out_shape=[jax.ShapeDtypeStruct((rows, hidden), BF)] * 2,
        compiler_params=params(),
        cost_estimate=cost(2 * rows * features * hidden, 17e6),
        name="hidden_grads",
    )(z, dy, *down, p, s)


def weight_kernel(shift_ref, a_ref, b_ref, out_ref):
    out_ref[...] = mm(a_ref[...], b_ref[...], ((0,), (0,))).astype(BF)


def weight_grad(shift, a, b, name):
    rows, features = a.shape
    hidden = b.shape[1]
    tile = features // ZN
    return pl.pallas_call(
        weight_kernel,
        grid_spec=pltpu.PrefetchScalarGridSpec(
            num_scalar_prefetch=1,
            grid=(ZN,),
            in_specs=[
                pl.BlockSpec((rows, tile), lambda i, shift: (0, (i + shift[0]) % ZN)),
                pl.BlockSpec((rows, hidden), lambda i, shift: (0, 0)),
            ],
            out_specs=pl.BlockSpec((tile, hidden), lambda i, shift: (i, 0)),
        ),
        out_shape=jax.ShapeDtypeStruct((features, hidden), BF),
        compiler_params=params(),
        cost_estimate=cost(2 * rows * features * hidden, 9e6),
        name=name,
    )(shift, a, b)


def ring_kernel(block_ref, first_ref, second_ref, b_ref, *out_refs):
    half = first_ref.shape[1]
    top = mm(first_ref[...], b_ref[...], ((0,), (0,))).astype(BF)
    low = mm(second_ref[...], b_ref[...], ((0,), (0,))).astype(BF)
    for k, out_ref in enumerate(out_refs):

        @pl.when(pl.program_id(0) == k)
        def _():
            out_ref[:half, :] = top
            out_ref[half:, :] = low


RING_PARTS = (((2, 0), (1, 1)), ((2, 1), (3, 0)), ((1, 0), (3, 1)), ((0, 0), (0, 1)))


def ring_grad(z, a, b, name):
    rows, features = a.shape
    hidden = b.shape[1]
    width = features // (2 * ZN)
    blocks = [(z + far) % ZN * 2 + r for pair in RING_PARTS for far, r in pair]
    part = pl.BlockSpec((2 * width, hidden), lambda i, blocks: (0, 0))
    return pl.pallas_call(
        ring_kernel,
        grid_spec=pltpu.PrefetchScalarGridSpec(
            num_scalar_prefetch=1,
            grid=(ZN,),
            in_specs=[
                pl.BlockSpec((rows, width), lambda i, blocks: (0, blocks[2 * i])),
                pl.BlockSpec((rows, width), lambda i, blocks: (0, blocks[2 * i + 1])),
                pl.BlockSpec((rows, hidden), lambda i, blocks: (0, 0)),
            ],
            out_specs=[part] * ZN,
        ),
        out_shape=[jax.ShapeDtypeStruct((2 * width, hidden), BF)] * ZN,
        compiler_params=params(),
        cost_estimate=cost(2 * rows * features * hidden, 9e6),
        name=name,
    )(jnp.concatenate(blocks), a, a, b)


def input_kernel(dg_ref, du_ref, gate_ref, up_ref, out_ref):
    acc = mm(dg_ref[...], gate_ref[...], ((1,), (1,)))
    acc = acc + mm(du_ref[...], up_ref[...], ((1,), (1,)))
    out_ref[...] = acc.astype(BF)


def input_grad(dg, du, gate_up):
    rows, hidden = dg.shape
    features = gate_up.shape[0]
    tile = 512
    left = pl.BlockSpec((rows, hidden), lambda i: (0, 0))
    gate = pl.BlockSpec((tile, hidden), lambda i: (i, 0))
    up = pl.BlockSpec((tile, hidden), lambda i: (i, 1))
    return pl.pallas_call(
        input_kernel,
        grid=(features // tile,),
        in_specs=[left, left, gate, up],
        out_specs=pl.BlockSpec((rows, tile), lambda i: (0, i)),
        out_shape=jax.ShapeDtypeStruct((rows, features), BF),
        compiler_params=params(),
        cost_estimate=cost(4 * rows * features * hidden, 14e6),
        name="input_grad",
    )(dg, du, gate_up, gate_up)


def adam_kernel(n_sums, keep_ref, *refs):
    w_ref, m_ref, v_ref, wb_ref, mb_ref, vb_ref = refs[n_sums : n_sums + 6]
    nw_ref, nm_ref, nv_ref = refs[-3:]
    keep = keep_ref[0] != 0
    grad = sum(ref[...].astype(F32) for ref in refs[:n_sums])
    w = jnp.where(keep, w_ref[...], wb_ref[...].astype(F32))
    m = jnp.where(keep, m_ref[...], mb_ref[...].astype(F32))
    v = jnp.where(keep, v_ref[...], vb_ref[...].astype(F32))
    m = 0.9 * m + 0.1 * grad
    v = 0.95 * v + 0.05 * grad * grad
    update = m / (1.0 - 0.9**10) / (jnp.sqrt(v / (1.0 - 0.95**10)) + 1e-08)
    nw_ref[...] = w - 0.003 * (update + 0.1 * w)
    nm_ref[...] = m
    nv_ref[...] = v


def adam(keep, sums, state, moved, k, before):
    rows, hidden = state[0].shape[0], sums[0][0].shape[1]
    tile = min(128, rows)
    steps = rows // tile
    column = pl.BlockSpec((tile, hidden), lambda i, keep: (i, k))
    shape = jax.ShapeDtypeStruct(state[0].shape, F32)

    def at(block):
        return pl.BlockSpec((tile, hidden), lambda i, keep: (i, block))

    def term(half):
        return pl.BlockSpec((tile, hidden), lambda i, keep: (i + half * steps, 0))

    return pl.pallas_call(
        functools.partial(adam_kernel, len(sums)),
        grid_spec=pltpu.PrefetchScalarGridSpec(
            num_scalar_prefetch=1,
            grid=(steps,),
            in_specs=[term(half) for _, half in sums]
            + [column] * 3
            + [at(block) for _, block in moved]
            + [pl.BlockSpec(memory_space=pl.ANY)] * len(before),
            out_specs=[column] * 3,
        ),
        out_shape=[shape] * 3,
        input_output_aliases={len(sums) + 7 + i: i for i in range(len(before))},
        compiler_params=params(),
        cost_estimate=cost(20 * rows * hidden, 34 * rows * hidden),
        name="adam",
    )(keep, *[v for v, _ in sums], *state, *[v for v, _ in moved], *before)


def per_device(tokens, cotangent, routes, owner, master, moment1, moment2):
    experts = lax.axis_size("expert")
    half = experts // 2
    position = lax.axis_index("expert")
    high = (lax.axis_index("dp") // ZN).astype(jnp.int32).reshape(1)
    keep = owner[position] == position
    info = keep.astype(jnp.int32).reshape(1)
    hidden = master.shape[2] // 3
    features = tokens.shape[2]
    count = tokens.shape[1]
    capacity = 2 * count // experts
    rows = experts * capacity
    replicas = lax.axis_size("dp")
    z_groups = [[h * ZN + z for z in range(ZN)] for h in range(replicas // ZN)]

    route_ids = routes[0, :, 0]
    columns = jnp.arange(experts, dtype=jnp.int32)
    onehot = (route_ids[:, None] == columns[None, :]).astype(jnp.int32)
    slot = jnp.sum((jnp.cumsum(onehot, axis=0) - 1) * onehot, axis=1)
    flat = route_ids * capacity + slot
    send_x = dispatch(high, flat, tokens[0], rows)
    send_dy = dispatch(high, flat, cotangent[0], rows)

    def over_owners(value):
        return permuted(value, "expert", lambda i: i ^ half)

    def over_high(value):
        return permuted(value, "dp", lambda i: i ^ ZN)

    def over_experts(value):
        boxes = value.reshape(experts, capacity, value.shape[1])
        out = lax.all_to_all(boxes, "expert", split_axis=0, concat_axis=0, tiled=True)
        return out.reshape(value.shape)

    def gathered(value):
        return lax.all_gather(value, "dp", axis=0, tiled=True, axis_index_groups=z_groups)

    def scattered(grad):
        return lax.psum_scatter(
            grad, "dp", scatter_dimension=0, tiled=True, axis_index_groups=z_groups
        )

    def to_next(value):
        return permuted(value, "dp", lambda i: i // ZN * ZN + (i + 1) % ZN)

    def to_last(value):
        return permuted(value, "dp", lambda i: i // ZN * ZN + (i - 1) % ZN)

    z = (lax.axis_index("dp") % ZN).astype(jnp.int32).reshape(1)
    nought = jnp.zeros((1,), jnp.int32)

    split = 2 * hidden
    own_a, own_b = master[0, :, :split].astype(BF), master[0, :, split:].astype(BF)
    other_a = over_owners(own_a)
    own_b, other_a = lax.optimization_barrier((own_b, other_a))
    other_b = over_owners(own_b)
    placed_a = lax.optimization_barrier(jnp.where(keep, own_a, other_a))
    far_a = over_high(placed_a)
    placed_a, far_a, other_b, send_x = lax.optimization_barrier((placed_a, far_a, other_b, send_x))
    gate_up = gathered(jnp.concatenate([placed_a, far_a], axis=0))
    x = over_experts(send_x)
    placed_b = jnp.where(keep, own_b, other_b)
    far_b = over_high(placed_b)
    down_own = jnp.concatenate([placed_b, far_b], axis=0)
    send_dy, x, down_own = lax.optimization_barrier((send_dy, x, down_own))
    dy = over_experts(send_dy)
    down_last, down_next = to_next(down_own), to_last(down_own)
    h, p, s = forward(x, gate_up)
    down_last, down_next, h = lax.optimization_barrier((down_last, down_next, h))
    quarter = down_own.shape[0] // 2
    down = (down_own, down_next, down_last, to_next(down_last[:quarter]), to_last(down_next[quarter:]))

    def ring_first(parts):
        return to_next(parts[0]), to_last(parts[1])

    def ring_second(parts, ahead, behind):
        size = ahead.shape[0] // 2
        top = parts[2][:size].astype(F32) + ahead[:size].astype(F32)
        low = parts[2][size:].astype(F32) + behind[:size].astype(F32)
        return to_next(top.astype(BF)), to_last(low.astype(BF))

    def ring_away(parts, ahead, behind, top, low):
        size = top.shape[0]
        away = parts[3][size:].astype(F32) + low.astype(F32) + ahead[size:].astype(F32)
        return away.astype(BF)

    def ring_near(parts, ahead, behind, top, low):
        return (parts[3], 0), (top, 0), (behind, 1)

    together = lax.optimization_barrier

    m_all, v_all = moment1[0].astype(BF), moment2[0].astype(BF)
    m_own = jnp.concatenate([m_all[:, :hidden], m_all[:, split:]], axis=1)
    v_own = [
        jnp.concatenate([v_all[:, split:], v_all[:, :hidden]], axis=1),
        jnp.concatenate([m_all[:, hidden:split], v_all[:, hidden:split]], axis=1),
    ]
    dy, m_own, *others = together((dy, m_own, *v_own, *down[3:]))
    v_own, down = others[:2], (*down[:3], *others[2:])
    part_down = scattered(weight_grad(nought, dy, h, "grad_down")).reshape(2, -1, hidden)
    m_other = over_owners(m_own)
    dg, du = hidden_grads(z, dy, down, p, s)
    send_back = input_grad(dg, du, gate_up)
    send_back, dg, du = together((send_back, dg, du))
    returned = over_experts(send_back)
    dg, du, m_other = together((dg, du, m_other))

    gate = ring_grad(z, x, dg, "grad_gate")
    gate, du = together((gate, du))
    first_gate = ring_first(gate)
    up = ring_grad(z, x, du, "grad_up")
    first_up = ring_first(up)
    first_gate, up, v_own = together((first_gate, up, v_own))
    second_gate = ring_second(gate, *first_gate)
    far_down = over_high(part_down[1])
    token_grad = combine(high, flat, returned, count)
    first_up, second_gate, far_down, token_grad = together(
        (first_up, second_gate, far_down, token_grad)
    )
    far_gate = over_high(ring_away(gate, *first_gate, *second_gate))
    v_other = [over_owners(v) for v in v_own]
    second_up = ring_second(up, *first_up)
    second_up, v_other[0] = together((second_up, v_other[0]))
    far_up = over_high(ring_away(up, *first_up, *second_up))

    state = (master[0], moment1[0], moment2[0])
    steps = (
        (2, ((part_down[0], 0), (far_down, 0)), ((other_b, 0), (m_other, 1), (v_other[0], 0))),
        (
            0,
            (*ring_near(gate, *first_gate, *second_gate), (far_gate, 0)),
            ((other_a, 0), (m_other, 0), (v_other[0], 1)),
        ),
        (
            1,
            (*ring_near(up, *first_up, *second_up), (far_up, 0)),
            ((other_a, 1), (v_other[1], 0), (v_other[1], 1)),
        ),
    )
    new = ()
    for k, sums, moved in steps:
        new = adam(info, sums, state, moved, k, new)
    return (token_grad[None], new[0][None], new[1][None], new[2][None])


def solution(mesh):
    placed = (
        P("dp", "expert", None),
        P("dp", "expert", None),
        P("dp", "expert", None),
        P(),
        P("expert", "dp", None),
        P("expert", "dp", None),
        P("expert", "dp", None),
    )
    return jax.shard_map(
        per_device,
        mesh=mesh,
        in_specs=placed,
        out_specs=(
            P("dp", "expert", None),
            P("expert", "dp", None),
            P("expert", "dp", None),
            P("expert", "dp", None),
        ),
        check_vma=False,
    )
```

```python
import functools
import jax
import jax.numpy as jnp
from jax import lax
from jax.experimental import pallas as pl
from jax.experimental.pallas import tpu as pltpu
from jax.sharding import PartitionSpec as P

BF = jnp.bfloat16
F32 = jnp.float32
VMEM_LIMIT = 56 * 1024 * 1024
ZN = 4


def params():
    return pltpu.CompilerParams(vmem_limit_bytes=VMEM_LIMIT)


def cost(flops, nbytes):
    return pl.CostEstimate(flops=int(flops), bytes_accessed=int(nbytes), transcendentals=0)


def permuted(value, axis, target):
    return lax.ppermute(value, axis, [(i, target(i)) for i in range(lax.axis_size(axis))])


def mm(a, b, dims):
    return lax.dot_general(a, b, (dims, ((), ())), preferred_element_type=F32)


def columns_of(i, high, width):
    other = high if i < ZN else 1 - high
    return pl.ds(pl.multiple_of(((i % ZN) * 2 + other) * width, width), width)


def dispatch_kernel(high_ref, flat_ref, tok_ref, out_ref):
    tile, features = out_ref.shape
    count = tok_ref.shape[0]
    width = features // (2 * ZN)
    ids = lax.broadcasted_iota(jnp.int32, (tile, count), 0) + pl.program_id(0) * tile
    onehot = (ids == flat_ref[...]).astype(F32).astype(BF)
    for i in range(2 * ZN):
        block = mm(onehot, tok_ref[:, i * width : (i + 1) * width], ((1,), (0,)))
        out_ref[:, columns_of(i, high_ref[0], width)] = block.astype(BF)


def dispatch(high, flat, tok, rows):
    count, features = tok.shape
    tile = min(512, rows)
    return pl.pallas_call(
        dispatch_kernel,
        grid_spec=pltpu.PrefetchScalarGridSpec(
            num_scalar_prefetch=1,
            grid=(rows // tile,),
            in_specs=[
                pl.BlockSpec((1, count), lambda i, high: (0, 0)),
                pl.BlockSpec((count, features), lambda i, high: (0, 0)),
            ],
            out_specs=pl.BlockSpec((tile, features), lambda i, high: (i, 0)),
        ),
        out_shape=jax.ShapeDtypeStruct((rows, features), BF),
        compiler_params=params(),
        cost_estimate=cost(2 * rows * count * features, 2 * features * (rows + count)),
        name="dispatch",
    )(high, flat.reshape(1, count), tok)


def combine_kernel(high_ref, flat_ref, back_ref, out_ref):
    rows, features = back_ref.shape
    width = features // (2 * ZN)
    ids = lax.broadcasted_iota(jnp.int32, (out_ref.shape[0], rows), 1)
    onehot = (ids == flat_ref[...]).astype(F32).astype(BF)
    for i in range(2 * ZN):
        block = mm(onehot, back_ref[:, columns_of(i, high_ref[0], width)], ((1,), (0,)))
        out_ref[:, i * width : (i + 1) * width] = block.astype(BF)


def combine(high, flat, back, count):
    rows, features = back.shape
    tile = min(256, count)
    return pl.pallas_call(
        combine_kernel,
        grid_spec=pltpu.PrefetchScalarGridSpec(
            num_scalar_prefetch=1,
            grid=(count // tile,),
            in_specs=[
                pl.BlockSpec((tile, 1), lambda i, high: (i, 0)),
                pl.BlockSpec((rows, features), lambda i, high: (0, 0)),
            ],
            out_specs=pl.BlockSpec((tile, features), lambda i, high: (i, 0)),
        ),
        out_shape=jax.ShapeDtypeStruct((count, features), BF),
        compiler_params=params(),
        cost_estimate=cost(2 * rows * count * features, 2 * features * (rows + count)),
        name="combine",
    )(high, flat.reshape(count, 1), back)


def forward_kernel(x_ref, gate_ref, up_ref, h_ref, p_ref, s_ref):
    x = x_ref[...]
    g = mm(x, gate_ref[...], ((1,), (0,)))
    u = mm(x, up_ref[...], ((1,), (0,)))
    sig = jax.nn.sigmoid(g)
    s = g * sig
    h_ref[...] = (s * u).astype(BF)
    p_ref[...] = u * sig * (1.0 + g * (1.0 - sig))
    s_ref[...] = s


def forward(x, gate_up):
    rows, features = x.shape
    hidden = gate_up.shape[1] // 2
    tile = min(256, hidden)
    tiles = hidden // tile
    out = pl.BlockSpec((rows, tile), lambda j: (0, j))
    return pl.pallas_call(
        forward_kernel,
        grid=(hidden // tile,),
        in_specs=[
            pl.BlockSpec((rows, features), lambda j: (0, 0)),
            pl.BlockSpec((features, tile), lambda j: (0, j)),
            pl.BlockSpec((features, tile), lambda j: (0, j + tiles)),
        ],
        out_specs=[out, out, out],
        out_shape=[
            jax.ShapeDtypeStruct((rows, hidden), BF),
            jax.ShapeDtypeStruct((rows, hidden), F32),
            jax.ShapeDtypeStruct((rows, hidden), F32),
        ],
        compiler_params=params(),
        cost_estimate=cost(4 * rows * features * hidden, 20e6),
        name="forward",
    )(x, gate_up, gate_up)


def hidden_kernel(z_ref, dy_ref, own_ref, next_ref, last_ref, top_ref, low_ref, p_ref, s_ref, dg_ref, du_ref):
    size = own_ref.shape[0]
    half = size // 2

    def part(away, start, ref):
        block = lax.rem(z_ref[0] + away, ZN)
        columns = pl.ds(pl.multiple_of(block * size + start, half), ref.shape[0])
        return mm(dy_ref[:, columns], ref[...], ((1,), (0,)))

    dh = part(0, 0, own_ref) + part(1, 0, next_ref) + part(ZN - 1, 0, last_ref)
    dh = dh + part(2, 0, top_ref) + part(2, half, low_ref)
    dg_ref[...] = (dh * p_ref[...]).astype(BF)
    du_ref[...] = (dh * s_ref[...]).astype(BF)


def hidden_grads(z, dy, down, p, s):
    rows, features = dy.shape
    hidden = p.shape[1]
    tile = min(256, rows)
    out = pl.BlockSpec((tile, hidden), lambda i, z: (i, 0))
    return pl.pallas_call(
        hidden_kernel,
        grid_spec=pltpu.PrefetchScalarGridSpec(
            num_scalar_prefetch=1,
            grid=(rows // tile,),
            in_specs=[pl.BlockSpec((tile, features), lambda i, z: (i, 0))]
            + [pl.BlockSpec(v.shape, lambda i, z: (0, 0)) for v in down]
            + [out, out],
            out_specs=[out, out],
        ),
        out_shape=[jax.ShapeDtypeStruct((rows, hidden), BF)] * 2,
        compiler_params=params(),
        cost_estimate=cost(2 * rows * features * hidden, 17e6),
        name="hidden_grads",
    )(z, dy, *down, p, s)


def weight_kernel(a_ref, b_ref, out_ref):
    out_ref[...] = mm(a_ref[...], b_ref[...], ((0,), (0,))).astype(BF)


def weight_grad(a, b, name):
    rows, features = a.shape
    hidden = b.shape[1]
    tile = features // 2
    return pl.pallas_call(
        weight_kernel,
        grid=(features // tile,),
        in_specs=[
            pl.BlockSpec((rows, tile), lambda i: (0, i)),
            pl.BlockSpec((rows, hidden), lambda i: (0, 0)),
        ],
        out_specs=pl.BlockSpec((tile, hidden), lambda i: (i, 0)),
        out_shape=jax.ShapeDtypeStruct((features, hidden), BF),
        compiler_params=params(),
        cost_estimate=cost(2 * rows * features * hidden, 9e6),
        name=name,
    )(a, b)


def ring_kernel(block_ref, first_ref, second_ref, b_ref, *out_refs):
    half = first_ref.shape[1]
    top = mm(first_ref[...], b_ref[...], ((0,), (0,))).astype(BF)
    low = mm(second_ref[...], b_ref[...], ((0,), (0,))).astype(BF)
    for k, out_ref in enumerate(out_refs):

        @pl.when(pl.program_id(0) == k)
        def _():
            out_ref[:half, :] = top
            out_ref[half:, :] = low


RING_PARTS = (((2, 0), (1, 1)), ((2, 1), (3, 0)), ((1, 0), (3, 1)), ((0, 0), (0, 1)))


def ring_grad(z, a, b, name):
    rows, features = a.shape
    hidden = b.shape[1]
    width = features // (2 * ZN)
    blocks = [(z + far) % ZN * 2 + r for pair in RING_PARTS for far, r in pair]
    part = pl.BlockSpec((2 * width, hidden), lambda i, blocks: (0, 0))
    return pl.pallas_call(
        ring_kernel,
        grid_spec=pltpu.PrefetchScalarGridSpec(
            num_scalar_prefetch=1,
            grid=(ZN,),
            in_specs=[
                pl.BlockSpec((rows, width), lambda i, blocks: (0, blocks[2 * i])),
                pl.BlockSpec((rows, width), lambda i, blocks: (0, blocks[2 * i + 1])),
                pl.BlockSpec((rows, hidden), lambda i, blocks: (0, 0)),
            ],
            out_specs=[part] * ZN,
        ),
        out_shape=[jax.ShapeDtypeStruct((2 * width, hidden), BF)] * ZN,
        compiler_params=params(),
        cost_estimate=cost(2 * rows * features * hidden, 9e6),
        name=name,
    )(jnp.concatenate(blocks), a, a, b)


def input_kernel(dg_ref, du_ref, gate_ref, up_ref, out_ref):
    acc = mm(dg_ref[...], gate_ref[...], ((1,), (1,)))
    acc = acc + mm(du_ref[...], up_ref[...], ((1,), (1,)))
    out_ref[...] = acc.astype(BF)


def input_grad(dg, du, gate_up):
    rows, hidden = dg.shape
    features = gate_up.shape[0]
    tile = 512
    left = pl.BlockSpec((rows, hidden), lambda i: (0, 0))
    gate = pl.BlockSpec((tile, hidden), lambda i: (i, 0))
    up = pl.BlockSpec((tile, hidden), lambda i: (i, 1))
    return pl.pallas_call(
        input_kernel,
        grid=(features // tile,),
        in_specs=[left, left, gate, up],
        out_specs=pl.BlockSpec((rows, tile), lambda i: (0, i)),
        out_shape=jax.ShapeDtypeStruct((rows, features), BF),
        compiler_params=params(),
        cost_estimate=cost(4 * rows * features * hidden, 14e6),
        name="input_grad",
    )(dg, du, gate_up, gate_up)


def adam_kernel(n_sums, keep_ref, *refs):
    w_ref, m_ref, v_ref, wb_ref, mb_ref, vb_ref = refs[n_sums : n_sums + 6]
    nw_ref, nm_ref, nv_ref = refs[-3:]
    keep = keep_ref[0] != 0
    grad = sum(ref[...].astype(F32) for ref in refs[:n_sums])
    w = jnp.where(keep, w_ref[...], wb_ref[...].astype(F32))
    m = jnp.where(keep, m_ref[...], mb_ref[...].astype(F32))
    v = jnp.where(keep, v_ref[...], vb_ref[...].astype(F32))
    m = 0.9 * m + 0.1 * grad
    v = 0.95 * v + 0.05 * grad * grad
    update = m / (1.0 - 0.9**10) / (jnp.sqrt(v / (1.0 - 0.95**10)) + 1e-08)
    nw_ref[...] = w - 0.003 * (update + 0.1 * w)
    nm_ref[...] = m
    nv_ref[...] = v


def adam(keep, sums, state, moved, k, before):
    rows, hidden = state[0].shape[0], sums[0][0].shape[1]
    tile = min(128, rows)
    steps = rows // tile
    column = pl.BlockSpec((tile, hidden), lambda i, keep: (i, k))
    shape = jax.ShapeDtypeStruct(state[0].shape, F32)

    def at(block):
        return pl.BlockSpec((tile, hidden), lambda i, keep: (i, block))

    def term(half):
        return pl.BlockSpec((tile, hidden), lambda i, keep: (i + half * steps, 0))

    return pl.pallas_call(
        functools.partial(adam_kernel, len(sums)),
        grid_spec=pltpu.PrefetchScalarGridSpec(
            num_scalar_prefetch=1,
            grid=(steps,),
            in_specs=[term(half) for _, half in sums]
            + [column] * 3
            + [at(block) for _, block in moved]
            + [pl.BlockSpec(memory_space=pl.ANY)] * len(before),
            out_specs=[column] * 3,
        ),
        out_shape=[shape] * 3,
        input_output_aliases={len(sums) + 7 + i: i for i in range(len(before))},
        compiler_params=params(),
        cost_estimate=cost(20 * rows * hidden, 34 * rows * hidden),
        name="adam",
    )(keep, *[v for v, _ in sums], *state, *[v for v, _ in moved], *before)


def per_device(tokens, cotangent, routes, owner, master, moment1, moment2):
    experts = lax.axis_size("expert")
    half = experts // 2
    position = lax.axis_index("expert")
    high = (lax.axis_index("dp") // ZN).astype(jnp.int32).reshape(1)
    keep = owner[position] == position
    info = keep.astype(jnp.int32).reshape(1)
    hidden = master.shape[2] // 3
    features = tokens.shape[2]
    count = tokens.shape[1]
    capacity = 2 * count // experts
    rows = experts * capacity
    replicas = lax.axis_size("dp")
    z_groups = [[h * ZN + z for z in range(ZN)] for h in range(replicas // ZN)]

    route_ids = routes[0, :, 0]
    columns = jnp.arange(experts, dtype=jnp.int32)
    onehot = (route_ids[:, None] == columns[None, :]).astype(jnp.int32)
    slot = jnp.sum((jnp.cumsum(onehot, axis=0) - 1) * onehot, axis=1)
    flat = route_ids * capacity + slot
    send_x = dispatch(high, flat, tokens[0], rows)
    send_dy = dispatch(high, flat, cotangent[0], rows)

    def over_owners(value):
        return permuted(value, "expert", lambda i: i ^ half)

    def over_high(value):
        return permuted(value, "dp", lambda i: i ^ ZN)

    def over_experts(value):
        boxes = value.reshape(experts, capacity, value.shape[1])
        out = lax.all_to_all(boxes, "expert", split_axis=0, concat_axis=0, tiled=True)
        return out.reshape(value.shape)

    def gathered(value):
        return lax.all_gather(value, "dp", axis=0, tiled=True, axis_index_groups=z_groups)

    def scattered(grad):
        return lax.psum_scatter(
            grad, "dp", scatter_dimension=0, tiled=True, axis_index_groups=z_groups
        )

    def to_next(value):
        return permuted(value, "dp", lambda i: i // ZN * ZN + (i + 1) % ZN)

    def to_last(value):
        return permuted(value, "dp", lambda i: i // ZN * ZN + (i - 1) % ZN)

    z = (lax.axis_index("dp") % ZN).astype(jnp.int32).reshape(1)

    split = 2 * hidden
    own_a, own_b = master[0, :, :split].astype(BF), master[0, :, split:].astype(BF)
    other_a = over_owners(own_a)
    own_b, other_a = lax.optimization_barrier((own_b, other_a))
    other_b = over_owners(own_b)
    placed_a = lax.optimization_barrier(jnp.where(keep, own_a, other_a))
    far_a = over_high(placed_a)
    placed_a, far_a, other_b, send_x = lax.optimization_barrier((placed_a, far_a, other_b, send_x))
    gate_up = gathered(jnp.concatenate([placed_a, far_a], axis=0))
    x = over_experts(send_x)
    placed_b = jnp.where(keep, own_b, other_b)
    far_b = over_high(placed_b)
    down_own = jnp.concatenate([placed_b, far_b], axis=0)
    send_dy, x, down_own = lax.optimization_barrier((send_dy, x, down_own))
    dy = over_experts(send_dy)
    down_last, down_next = to_next(down_own), to_last(down_own)
    h, p, s = forward(x, gate_up)
    down_last, down_next, h = lax.optimization_barrier((down_last, down_next, h))
    quarter = down_own.shape[0] // 2
    down = (down_own, down_next, down_last, to_next(down_last[:quarter]), to_last(down_next[quarter:]))

    def ring_first(parts):
        return to_next(parts[0]), to_last(parts[1])

    def ring_second(parts, ahead, behind):
        size = ahead.shape[0] // 2
        top = parts[2][:size].astype(F32) + ahead[:size].astype(F32)
        low = parts[2][size:].astype(F32) + behind[:size].astype(F32)
        return to_next(top.astype(BF)), to_last(low.astype(BF))

    def ring_away(parts, ahead, behind, top, low):
        size = top.shape[0]
        away = parts[3][size:].astype(F32) + low.astype(F32) + ahead[size:].astype(F32)
        return away.astype(BF)

    def ring_near(parts, ahead, behind, top, low):
        return (parts[3], 0), (top, 0), (behind, 1)

    together = lax.optimization_barrier

    m_all, v_all = moment1[0].astype(BF), moment2[0].astype(BF)
    m_own = jnp.concatenate([m_all[:, :hidden], m_all[:, split:]], axis=1)
    v_own = [
        jnp.concatenate([v_all[:, split:], v_all[:, :hidden]], axis=1),
        jnp.concatenate([m_all[:, hidden:split], v_all[:, hidden:split]], axis=1),
    ]
    dy, m_own, *others = together((dy, m_own, *v_own, *down[3:]))
    v_own, down = others[:2], (*down[:3], *others[2:])
    part_down = scattered(weight_grad(dy, h, "grad_down")).reshape(2, -1, hidden)
    m_other = over_owners(m_own)
    dg, du = hidden_grads(z, dy, down, p, s)
    send_back = input_grad(dg, du, gate_up)
    send_back, m_other, dg, du = together((send_back, m_other, dg, du))
    returned = over_experts(send_back)

    gate = ring_grad(z, x, dg, "grad_gate")
    gate, du = together((gate, du))
    first_gate = ring_first(gate)
    up = ring_grad(z, x, du, "grad_up")
    first_up = ring_first(up)
    first_gate, up, v_own = together((first_gate, up, v_own))
    second_gate = ring_second(gate, *first_gate)
    far_down = over_high(part_down[1])
    token_grad = combine(high, flat, returned, count)
    first_up, second_gate, far_down, token_grad = together(
        (first_up, second_gate, far_down, token_grad)
    )
    far_gate = over_high(ring_away(gate, *first_gate, *second_gate))
    v_other = [over_owners(v) for v in v_own]
    second_up = ring_second(up, *first_up)
    second_up, v_other[0] = together((second_up, v_other[0]))
    far_up = over_high(ring_away(up, *first_up, *second_up))

    state = (master[0], moment1[0], moment2[0])
    steps = (
        (2, ((part_down[0], 0), (far_down, 0)), ((other_b, 0), (m_other, 1), (v_other[0], 0))),
        (
            0,
            (*ring_near(gate, *first_gate, *second_gate), (far_gate, 0)),
            ((other_a, 0), (m_other, 0), (v_other[0], 1)),
        ),
        (
            1,
            (*ring_near(up, *first_up, *second_up), (far_up, 0)),
            ((other_a, 1), (v_other[1], 0), (v_other[1], 1)),
        ),
    )
    new = ()
    for k, sums, moved in steps:
        new = adam(info, sums, state, moved, k, new)
    return (token_grad[None], new[0][None], new[1][None], new[2][None])


def solution(mesh):
    placed = (
        P("dp", "expert", None),
        P("dp", "expert", None),
        P("dp", "expert", None),
        P(),
        P("expert", "dp", None),
        P("expert", "dp", None),
        P("expert", "dp", None),
    )
    return jax.shard_map(
        per_device,
        mesh=mesh,
        in_specs=placed,
        out_specs=(
            P("dp", "expert", None),
            P("expert", "dp", None),
            P("expert", "dp", None),
            P("expert", "dp", None),
        ),
        check_vma=False,
    )
```
